512 devices in a mesh: layer: 8 (over z_lo, core), feat: 64 (over y, x, z_hi).
Axes of the slice: x: 4, y: 4, z: 16 (z_hi: 4, z_lo: 4; z = z_hi * 4 + z_lo), core: 2. Of those that a mesh axis runs over, the one named last changes fastest.
Arguments:
- acts: bfloat16 [960, 3584], P('feat', 'layer'), may hold values from -48 to 48, as said below
- enc_weight: bfloat16 [3584, 32768], P('layer', 'feat'), may hold values from -0.09375 to 0.09375
- enc_bias: float32 [32768], P('feat'), may hold values from -3 to 3
- dec_weight: bfloat16 [32768, 3584], P('feat', 'layer'), as said below
- dec_bias: float32 [3584], P('layer'), may hold values from -3 to 3
- enc_moment: float32 [3584, 32768], P('layer', 'feat'), may hold values from -0.06 to 0.06
- enc_second: float32 [3584, 32768], P('layer', 'feat'), may hold values from 1e-05 to 0.001
Outputs:
- enc_new: bfloat16 [3584, 32768], P('layer', 'feat')
- moment_new: float32 [3584, 32768], P('layer', 'feat')
- second_new: float32 [3584, 32768], P('layer', 'feat')
- total_loss: float32 [], replicated
The draws below stay inside these ranges and needn't reach their ends.
Inputs may be any that keep to these rules, and one draw needn't show every extreme that they name: `acts`: activations with token scales and channel scales that vary. `dec_weight`: decoder rows with scales that vary over latents and layers.
All inputs are finite; a program needn't handle non-finite values.
Results may differ from the reference program's by a relative error of at most 0.0051.
Values may be sent and summed in bfloat16 or wider, within the bound.
No kernel may reach another device: no remote copies, remote signals or barrier semaphores. Data moves between devices by JAX's collectives and lax.ppermute only.
A program may use at most 64 MiB of HBM per device.

```python
import math
import jax
import jax.numpy as jnp
from jax import lax

D = 1792
LAYERS = 2
BATCH = 960
CHANNELS = 3584
LATENTS = 32768


def draw_acts(key, part):
    key = jax.random.fold_in(key, 11)
    key_base = jax.random.fold_in(key, 1)
    key_rows = jax.random.fold_in(key, 2)
    key_cols = jax.random.fold_in(key, 3)
    ramp = jnp.arange(BATCH, dtype=jnp.float32) / max(BATCH - 1, 1)
    row_scale = jnp.exp(0.55 * ramp + 2.3 * jax.random.uniform(key_rows, (BATCH,), jnp.float32) - 1.5)
    col_scale = jnp.exp(1.2 * jax.random.uniform(key_cols, (LAYERS, D), jnp.float32) - 0.6)
    base = jnp.clip(jax.random.normal(key_base, (BATCH, LAYERS, D), jnp.float32), -6.0, 6.0)
    full = base * row_scale[:, None, None] * col_scale[None, :, :]
    return full.reshape(BATCH, LAYERS * D).astype(jnp.bfloat16)


def draw_dec_weight(key, part):
    key = jax.random.fold_in(key, 23)
    key_base = jax.random.fold_in(key, 1)
    key_lat = jax.random.fold_in(key, 2)
    lat_scale = jnp.exp(2.3 * jax.random.uniform(key_lat, (LATENTS, 1, 1), jnp.float32) - 1.15)
    ramp = jnp.arange(LAYERS, dtype=jnp.float32) / max(LAYERS - 1, 1)
    lay_scale = jnp.exp(ramp * 1.0986123 - 0.5493061).reshape(1, LAYERS, 1)
    base = jnp.clip(jax.random.normal(key_base, (LATENTS, LAYERS, D), jnp.float32), -6.0, 6.0)
    full = base * lat_scale * lay_scale * LATENTS ** (-0.5)
    return full.reshape(LATENTS, LAYERS * D).astype(jnp.bfloat16)


def levels(own_key, shape, shards, least, largest):
    def one(dim, blocks):
        steps = jax.random.uniform(jax.random.fold_in(jax.random.fold_in(own_key, 6), dim), (blocks,), jnp.float32, least / len(shards), largest / len(shards))
        return jnp.repeat(jnp.exp(steps), shape[dim] // blocks).reshape((-1,) + (1,) * (len(shape) - dim - 1))

    level = one(*shards[0])
    for cut in shards[1:]:
        level = level * one(*cut)
    return level


def scatter_about(own_key, shape, width, reach, cuts=(), kind=jnp.bfloat16):
    entries = jax.random.normal(own_key, shape, jnp.float32) * width
    if len(cuts) > 0:
        entries = levels(own_key, shape, cuts, -0.22, 0.18) * entries
    return jnp.clip(entries, min=-reach, max=reach).astype(kind)


def setup_inputs(seed: int = 0) -> dict:
    key_of = jax.random.split(jax.random.key(seed), 8)
    acts = draw_acts(jax.random.fold_in(key_of[7], 71), 0)
    enc_weight = scatter_about(key_of[1], (CHANNELS, LATENTS), CHANNELS ** -0.5, 0.09375, ((0, 8), (1, 64)))
    enc_bias = scatter_about(key_of[2], (LATENTS,), 0.5, 3.0, ((0, 64),), jnp.float32)
    dec_weight = draw_dec_weight(jax.random.fold_in(key_of[7], 71), 0)
    dec_bias = scatter_about(key_of[4], (CHANNELS,), 0.5, 3.0, ((0, 8),), jnp.float32)
    enc_moment = scatter_about(key_of[5], (CHANNELS, LATENTS), 0.01, 0.06, ((0, 8), (1, 64)), jnp.float32)
    enc_second = jnp.clip(jnp.exp(math.log(0.001) - 4.6051703 * jax.random.uniform(key_of[6], (CHANNELS, LATENTS), jnp.float32) ** levels(key_of[6], (CHANNELS, LATENTS), ((0, 8), (1, 64)), -0.2, 0.2)), 9.999999747378752e-06, 0.001)
    return {"acts": acts, "enc_weight": enc_weight, "enc_bias": enc_bias, "dec_weight": dec_weight, "dec_bias": dec_bias, "enc_moment": enc_moment, "enc_second": enc_second}


sparsity = 0.5
beta_one = 0.9
beta_two = 0.999
first_fix = 0.9999734386011124
second_fix = 0.0952078528862911
learn_rate = 0.002
adam_eps = 1e-08
sharpness = 4.0

def reference(acts, enc_weight, enc_bias, dec_weight, dec_bias, enc_moment, enc_second):
    batch_rows = acts.shape[0]
    inv_batch = 1.0 / batch_rows
    lat_total = enc_weight.shape[1]
    preact = jnp.dot(acts, enc_weight, preferred_element_type=jnp.float32) + enc_bias
    codes = (jax.nn.softplus(sharpness * preact) / sharpness).astype(jnp.bfloat16)
    rebuilt = jnp.dot(codes, dec_weight, preferred_element_type=jnp.float32) + dec_bias.reshape(1, -1)
    error = rebuilt - acts.astype(jnp.float32)
    shaped = dec_weight.astype(jnp.float32).reshape(lat_total, LAYERS, D)
    dec_norms = lax.optimization_barrier(jnp.sum(jnp.sqrt(lax.optimization_barrier(jnp.sum(jnp.square(shaped), axis=2))), axis=1))
    code_sums = lax.optimization_barrier(jnp.sum(codes.astype(jnp.float32), axis=0))
    total_loss = inv_batch * (jnp.sum(error * error) + sparsity * jnp.sum(code_sums * dec_norms))
    grad_rebuilt = (error * (2.0 * inv_batch)).astype(jnp.bfloat16)
    code_grad = jnp.dot(grad_rebuilt, dec_weight.T, preferred_element_type=jnp.float32) + sparsity * inv_batch * dec_norms
    pre_grad = (code_grad * jax.nn.sigmoid(sharpness * preact)).astype(jnp.bfloat16)
    gradient = jnp.dot(acts.T, pre_grad, preferred_element_type=jnp.float32)
    moment_new = beta_one * enc_moment + (1.0 - beta_one) * gradient
    second_new = beta_two * enc_second + (1.0 - beta_two) * gradient * gradient
    update = moment_new / first_fix / (jnp.sqrt(second_new / second_fix) + adam_eps)
    enc_new = (enc_weight.astype(jnp.float32) - learn_rate * update).astype(jnp.bfloat16)
    return (enc_new, moment_new, second_new, total_loss)
```

```python
import jax
import jax.numpy as jnp
from jax import lax
from jax.sharding import Mesh, PartitionSpec as P

D = 1792
LAYERS = 2

sparsity = 0.5
beta_one = 0.9
beta_two = 0.999
first_fix = 0.9999734386011124
second_fix = 0.0952078528862911
learn_rate = 0.002
adam_eps = 1e-08
sharpness = 4.0

SIZES = (4, 2, 4, 4, 4)
NAMES = ("zl", "core", "y", "x", "zh")
LAYER = ("zl", "core")
FEAT = ("y", "x", "zh")
PLANE = ("y", "x")
PARTS = 8
BLOCKS = 16
HIGH = 4
BF = jnp.bfloat16
F32 = jnp.float32


def pieces(value):
    top = value.astype(BF)
    rest = value - top.astype(F32)
    mid = rest.astype(BF)
    low = (rest - mid.astype(F32)).astype(BF)
    return top, mid, low


def body(acts, enc_weight, enc_bias, dec_weight, dec_bias, enc_moment, enc_second):
    rows, chans = acts.shape
    latents = enc_weight.shape[1]
    inv_batch = 1.0 / (rows * BLOCKS * HIGH)
    wide = PARTS * chans
    part = lax.axis_index(LAYER)
    padded = rows + 1
    share = padded // PARTS

    enc_all = lax.all_gather(enc_weight, LAYER, axis=0, tiled=True)
    dec_all = lax.all_gather(dec_weight, LAYER, axis=0)

    bias_rows = jnp.stack(pieces(dec_bias))
    packed = jnp.concatenate([acts, jnp.zeros((1, chans), BF), bias_rows], axis=0)
    column = lax.all_gather(packed, ("zh",) + LAYER, axis=0)
    column = column.reshape(HIGH, PARTS, padded + 3, chans)
    bias_full = column[0, :, padded:].astype(F32).sum(axis=1).reshape(1, wide)
    mine = lax.dynamic_slice_in_dim(column[:, :, :padded], part * share, share, axis=2)
    mine = mine.transpose(0, 2, 1, 3).reshape(HIGH * share, wide)
    own = lax.dynamic_slice_in_dim(column[:, :, :padded], part, 1, axis=1)
    own = own.reshape(HIGH, PARTS, share, chans).transpose(1, 0, 2, 3)
    own = own.reshape(PARTS * HIGH * share, chans)

    small = HIGH * share
    tokens = BLOCKS * small
    acts_part = lax.all_gather(mine, PLANE, axis=0, tiled=True)

    preact = jnp.dot(acts_part, enc_all, preferred_element_type=F32) + enc_bias
    codes = (jax.nn.softplus(sharpness * preact) / sharpness).astype(BF)
    slopes = jax.nn.sigmoid(sharpness * preact)

    squares = jnp.sum(jnp.square(dec_all.astype(F32)), axis=2)
    per_layer = squares.reshape(LAYERS, PARTS // LAYERS, latents).sum(axis=1)
    dec_norms = jnp.sum(jnp.sqrt(per_layer), axis=0)

    sparse = jnp.sum(codes.astype(F32) * dec_norms, axis=1, keepdims=True)
    partial_value = jnp.einsum("bf,lfc->blc", codes, dec_all, preferred_element_type=F32)
    tail = jnp.zeros((tokens, 125), BF)
    sending = jnp.concatenate(
        [partial_value.reshape(tokens, wide).astype(BF), *pieces(sparse), tail], axis=1
    )
    got = lax.all_to_all(
        sending.reshape(BLOCKS, small, wide + 128), PLANE, 0, 0, tiled=True
    )
    summed = jnp.sum(got.astype(F32), axis=0)
    top = summed.astype(BF)
    again = lax.all_gather(top, "zh", axis=0)
    total = jnp.sum(again.astype(F32), axis=0)

    slots = part * share + jnp.arange(small, dtype=jnp.int32) % share
    real = (slots < rows).astype(F32)[:, None]
    error = total[:, :wide] + bias_full - mine.astype(F32)
    sparse_sum = jnp.sum(total[:, wide:], axis=1, keepdims=True)
    token_loss = real * inv_batch * (
        jnp.sum(error * error, axis=1, keepdims=True) + sparsity * sparse_sum
    )
    grad = (error * (2.0 * inv_batch)).astype(BF)
    grad_send = jnp.concatenate([grad, *pieces(token_loss), jnp.zeros((small, 125), BF)], axis=1)
    grad_got = lax.all_gather(grad_send, PLANE, axis=0, tiled=True)
    part_loss = jnp.sum(grad_got[:, wide:].astype(F32))
    grad_all = grad_got[:, :wide].reshape(tokens, PARTS, chans)
    code_grad = jnp.einsum("blc,lfc->bf", grad_all, dec_all, preferred_element_type=F32)
    code_grad = code_grad + sparsity * inv_batch * dec_norms
    pre_grad = (code_grad * slopes).astype(BF)

    loss_rows = jnp.broadcast_to(jnp.stack(pieces(part_loss))[:, None], (3, latents))
    last = jnp.concatenate([pre_grad, loss_rows, jnp.zeros((5, latents), BF)], axis=0)
    last_got = lax.all_gather(last, LAYER, axis=0)
    total_loss = jnp.sum(last_got[:, tokens : tokens + 3, 0].astype(F32))
    pre_all = last_got[:, :tokens]

    own_all = lax.all_gather(own, PLANE, axis=0)
    own_all = own_all.reshape(BLOCKS, PARTS, small, chans).transpose(1, 0, 2, 3)
    gradient = jnp.einsum(
        "lbc,lbf->cf",
        own_all.reshape(PARTS, tokens, chans),
        pre_all,
        preferred_element_type=F32,
    )
    moment_new = beta_one * enc_moment + (1.0 - beta_one) * gradient
    second_new = beta_two * enc_second + (1.0 - beta_two) * gradient * gradient
    update = moment_new / first_fix / (jnp.sqrt(second_new / second_fix) + adam_eps)
    enc_new = (enc_weight.astype(F32) - learn_rate * update).astype(BF)
    return (enc_new, moment_new, second_new, total_loss)


def solution(mesh):
    fine = Mesh(mesh.devices.reshape(SIZES), NAMES)
    return jax.shard_map(
        body,
        mesh=fine,
        in_specs=(
            P(FEAT, LAYER),
            P(LAYER, FEAT),
            P(FEAT),
            P(FEAT, LAYER),
            P(LAYER),
            P(LAYER, FEAT),
            P(LAYER, FEAT),
        ),
        out_specs=(P(LAYER, FEAT), P(LAYER, FEAT), P(LAYER, FEAT), P()),
        check_vma=False,
    )
```

```python
import jax
import jax.numpy as jnp
from jax import lax
from jax.sharding import Mesh, PartitionSpec as P

D = 1792
LAYERS = 2

sparsity = 0.5
beta_one = 0.9
beta_two = 0.999
first_fix = 0.9999734386011124
second_fix = 0.0952078528862911
learn_rate = 0.002
adam_eps = 1e-08
sharpness = 4.0

SIZES = (4, 2, 4, 4, 4)
NAMES = ("zl", "core", "y", "x", "zh")
LAYER = ("zl", "core")
FEAT = ("y", "x", "zh")
PLANE = ("y", "x")
CORES = 2
CHIPS = 4
PARTS = 8
BLOCKS = 16
HIGH = 4
LANES = 128
BF = jnp.bfloat16
F32 = jnp.float32


def pieces(value):
    top = value.astype(BF)
    rest = value - top.astype(F32)
    mid = rest.astype(BF)
    low = (rest - mid.astype(F32)).astype(BF)
    return top, mid, low


def spread(value, axes, count):
    copies = jnp.broadcast_to(value[None], (count,) + value.shape)
    return lax.all_to_all(copies, axes, 0, 0, tiled=True)


def swap(value):
    return lax.ppermute(value, "core", [(0, 1), (1, 0)])


def beside(value, number):
    rows = value.shape[0]
    lane = lax.broadcasted_iota(jnp.int32, (rows, LANES), 1)
    row = lax.broadcasted_iota(jnp.int32, (rows, LANES), 0)
    top, mid, low = pieces(number)
    zero = jnp.zeros((), BF)
    block = jnp.where(lane == 0, top, jnp.where(lane == 1, mid, jnp.where(lane == 2, low, zero)))
    return jnp.concatenate([value, jnp.where(row == 0, block, zero)], axis=1)


def body(acts, enc_weight, enc_bias, dec_weight, dec_bias, enc_moment, enc_second):
    rows, chans = acts.shape
    latents = enc_weight.shape[1]
    inv_batch = 1.0 / (rows * BLOCKS * HIGH)
    wide = PARTS * chans
    core = lax.axis_index("core")
    part = lax.axis_index(LAYER)
    padded = rows + 1
    share = padded // PARTS
    small = HIGH * share
    tokens = BLOCKS * small

    dec_all = lax.all_gather(dec_weight.T, LAYER, axis=0, tiled=True)

    packed = jnp.concatenate([acts, jnp.zeros((1, chans), BF)], axis=0)
    column = spread(packed, "zh", HIGH)
    column = column.reshape(HIGH, CHIPS, CORES, share, chans).transpose(2, 1, 0, 3, 4)
    column = column.reshape(PARTS, small, chans)
    gathered = spread(column, PLANE, BLOCKS).transpose(1, 0, 2, 3)
    gathered = gathered.reshape(CORES, CHIPS * tokens, chans)
    acts_here = lax.dynamic_index_in_dim(gathered, core, 0, keepdims=False)
    acts_there = lax.dynamic_index_in_dim(gathered, 1 - core, 0, keepdims=False)

    bias_rows = jnp.concatenate(
        [jnp.stack(pieces(dec_bias)), jnp.zeros((small - 3, chans), BF)], axis=0
    )
    by_part = column.reshape(CORES, CHIPS, small, chans).transpose(1, 0, 2, 3)
    by_part = by_part.reshape(PARTS, small, chans)
    small_send = jnp.concatenate(
        [by_part, jnp.broadcast_to(bias_rows[None], by_part.shape)], axis=1
    )
    small_got = lax.all_to_all(small_send, LAYER, 0, 0, tiled=True)
    mine = small_got[:, :small].transpose(1, 0, 2).reshape(small, wide).astype(F32)
    bias_full = small_got[:, small:].astype(F32).sum(axis=1).reshape(1, wide)

    sent = swap(jnp.dot(acts_there, enc_weight, preferred_element_type=F32))
    pair = jnp.dot(acts_here, enc_weight, preferred_element_type=F32) + sent
    quarter = lax.all_to_all(
        pair.astype(BF).reshape(CHIPS, tokens, latents), "zl", 0, 0, tiled=True
    )
    preact = jnp.sum(quarter.astype(F32), axis=0) + enc_bias
    codes = (jax.nn.softplus(sharpness * preact) / sharpness).astype(BF)
    slopes = jax.nn.sigmoid(sharpness * preact)

    squares = jnp.square(dec_all.astype(F32)).reshape(LAYERS, wide // LAYERS, latents)
    dec_norms = jnp.sum(jnp.sqrt(jnp.sum(squares, axis=1)), axis=0)

    def real(count):
        place = lax.broadcasted_iota(jnp.int32, (count, 1), 0) % share
        return (part * share + place < rows).astype(F32)

    sparse = jnp.sum(real(tokens) * codes.astype(F32) * dec_norms)
    partial_value = lax.dot_general(
        codes, dec_all, (((1,), (1,)), ((), ())), preferred_element_type=F32
    )
    got = lax.all_to_all(
        partial_value.astype(BF).reshape(BLOCKS, small, wide), PLANE, 0, 0, tiled=True
    )
    summed = jnp.sum(got.astype(F32), axis=0).astype(BF)
    total = jnp.sum(spread(beside(summed, sparse), "zh", HIGH).astype(F32), axis=0)

    error = total[:, :wide] + bias_full - mine
    piece = jnp.sum(real(small) * error * error) + sparsity * jnp.sum(total[:, wide:])
    grad = (error * (2.0 * inv_batch)).astype(BF)
    grad_got = spread(beside(grad, inv_batch * piece), PLANE, BLOCKS)
    grad_got = grad_got.reshape(tokens, wide + LANES)
    part_loss = jnp.sum(grad_got[:, wide:].astype(F32))
    code_grad = jnp.dot(grad_got[:, :wide], dec_all, preferred_element_type=F32)
    code_grad = code_grad + sparsity * inv_batch * dec_norms
    pre_grad = (code_grad * slopes).astype(BF)

    loss_rows = jnp.broadcast_to(jnp.stack(pieces(part_loss))[:, None], (3, latents))
    last = jnp.concatenate([pre_grad, loss_rows, jnp.zeros((5, latents), BF)], axis=0)
    pre_here = lax.all_gather(last, "zl", axis=0)
    pre_there = swap(pre_here)

    def part_of(acts_half, pre_half):
        return lax.dot_general(
            acts_half,
            pre_half[:, :tokens].reshape(CHIPS * tokens, latents),
            (((0,), (0,)), ((), ())),
            preferred_element_type=F32,
        )

    near, far = pre_here[:, tokens:, 0].astype(F32), pre_there[:, tokens:, 0].astype(F32)
    first, second = jnp.where(core == 0, near, far), jnp.where(core == 0, far, near)
    total_loss = jnp.sum(jnp.concatenate([first, second]))
    gradient = part_of(acts_here, pre_here) + part_of(acts_there, pre_there)
    moment_new = beta_one * enc_moment + (1.0 - beta_one) * gradient
    second_new = beta_two * enc_second + (1.0 - beta_two) * gradient * gradient
    update = moment_new / first_fix / (jnp.sqrt(second_new / second_fix) + adam_eps)
    enc_new = (enc_weight.astype(F32) - learn_rate * update).astype(BF)
    return (enc_new, moment_new, second_new, total_loss)


def solution(mesh):
    fine = Mesh(mesh.devices.reshape(SIZES), NAMES)
    return jax.shard_map(
        body,
        mesh=fine,
        in_specs=(
            P(FEAT, LAYER),
            P(LAYER, FEAT),
            P(FEAT),
            P(FEAT, LAYER),
            P(LAYER),
            P(LAYER, FEAT),
            P(LAYER, FEAT),
        ),
        out_specs=(P(LAYER, FEAT), P(LAYER, FEAT), P(LAYER, FEAT), P()),
        check_vma=False,
    )
```

```python
import jax
import jax.numpy as jnp
from jax import lax
from jax.sharding import Mesh, PartitionSpec as P

D = 1792
LAYERS = 2

sparsity = 0.5
beta_one = 0.9
beta_two = 0.999
first_fix = 0.9999734386011124
second_fix = 0.0952078528862911
learn_rate = 0.002
adam_eps = 1e-08
sharpness = 4.0

SIZES = (4, 2, 4, 4, 4)
NAMES = ("zl", "core", "y", "x", "zh")
LAYER = ("zl", "core")
FEAT = ("y", "x", "zh")
PLANE = ("y", "x")
CORES = 2
CHIPS = 4
PARTS = 8
BLOCKS = 16
HIGH = 4
LANES = 128
BF = jnp.bfloat16
F32 = jnp.float32


def pieces(value):
    top = value.astype(BF)
    rest = value - top.astype(F32)
    mid = rest.astype(BF)
    low = (rest - mid.astype(F32)).astype(BF)
    return top, mid, low


def spread(value, axes, count):
    copies = jnp.broadcast_to(value[None], (count,) + value.shape)
    return lax.all_to_all(copies, axes, 0, 0, tiled=True)


def swap(value):
    return lax.ppermute(value, "core", [(0, 1), (1, 0)])


def beside(value, number):
    rows = value.shape[0]
    lane = lax.broadcasted_iota(jnp.int32, (rows, LANES), 1)
    row = lax.broadcasted_iota(jnp.int32, (rows, LANES), 0)
    top, mid, low = pieces(number)
    zero = jnp.zeros((), BF)
    block = jnp.where(lane == 0, top, jnp.where(lane == 1, mid, jnp.where(lane == 2, low, zero)))
    return jnp.concatenate([value, jnp.where(row == 0, block, zero)], axis=1)


def body(acts, enc_weight, enc_bias, dec_weight, dec_bias, enc_moment, enc_second):
    rows, chans = acts.shape
    latents = enc_weight.shape[1]
    inv_batch = 1.0 / (rows * BLOCKS * HIGH)
    wide = PARTS * chans
    core = lax.axis_index("core")
    chip = lax.axis_index("zl")
    share = (rows + 1) // PARTS
    half = CHIPS * share
    small = HIGH * share
    tokens = BLOCKS * small

    dec_all = lax.all_gather(dec_weight.T, LAYER, axis=0, tiled=True)
    enc_there = swap(enc_weight)

    padded = jnp.concatenate([acts, jnp.zeros((1, chans), BF)], axis=0)
    bias_rows = jnp.stack(pieces(dec_bias))
    fill = jnp.zeros((half - 3, chans), BF)
    low, high = padded[:half], padded[half:]
    give = jnp.concatenate([jnp.where(core == 0, high, low), bias_rows, fill], axis=0)
    taken = swap(give)
    pair = jnp.concatenate([jnp.where(core == 0, low, high), taken[:half]], axis=1)
    column = spread(pair, "zh", HIGH).reshape(HIGH, CHIPS, share, 2 * chans)
    column = column.transpose(1, 0, 2, 3).reshape(CHIPS, small, 2 * chans)
    gathered = spread(column, PLANE, BLOCKS).transpose(1, 0, 2, 3)
    gathered = gathered.reshape(CHIPS * tokens, 2 * chans)
    acts_here = gathered[:, :chans]
    acts_there = swap(gathered[:, chans:])

    enc_pair = jnp.concatenate([enc_weight, enc_there], axis=0)
    sums = jnp.dot(gathered, enc_pair, preferred_element_type=F32).astype(BF)

    extra = jnp.concatenate(
        [
            column[:, :, :chans],
            column[:, :, chans:],
            jnp.broadcast_to(bias_rows[None], (CHIPS, 3, chans)),
            jnp.broadcast_to(taken[None, half : half + 3], (CHIPS, 3, chans)),
            jnp.zeros((CHIPS, 2, chans), BF),
        ],
        axis=1,
    )
    extra = jnp.pad(extra, ((0, 0), (0, 0), (0, latents - chans)))
    sending = jnp.concatenate([sums.reshape(CHIPS, tokens, latents), extra], axis=1)
    quarter = lax.all_to_all(sending, "zl", 0, 0, tiled=True)
    preact = jnp.sum(quarter[:, :tokens].astype(F32), axis=0) + enc_bias
    codes = (jax.nn.softplus(sharpness * preact) / sharpness).astype(BF)
    codes, acts_there = lax.optimization_barrier((codes, acts_there))
    slopes = jax.nn.sigmoid(sharpness * preact)

    def ordered(near, far):
        first, second = jnp.where(core == 0, near, far), jnp.where(core == 0, far, near)
        both = jnp.stack([first, second], axis=1)
        return both.transpose(2, 0, 1, 3).reshape(both.shape[2], wide)

    beyond = quarter[:, tokens:, :chans].astype(F32)
    mine = ordered(beyond[:, :small], beyond[:, small : 2 * small])
    end = 2 * small
    bias_near = beyond[:, end : end + 3].sum(axis=1, keepdims=True)
    bias_far = beyond[:, end + 3 : end + 6].sum(axis=1, keepdims=True)
    target = mine - ordered(bias_near, bias_far)

    partial_value = lax.dot_general(
        codes, dec_all, (((1,), (1,)), ((), ())), preferred_element_type=F32
    )
    dec_norms = jnp.zeros((latents,), F32)
    for layer in range(LAYERS):
        block = dec_all[layer * (wide // LAYERS) : (layer + 1) * (wide // LAYERS)].astype(F32)
        dec_norms = dec_norms + jnp.sqrt(jnp.sum(block * block, axis=0))

    def real(count):
        place = lax.broadcasted_iota(jnp.int32, (count, 1), 0) % share
        return (core * half + chip * share + place < rows).astype(F32)

    sparse = jnp.sum(real(tokens) * codes.astype(F32) * dec_norms)
    got = lax.all_to_all(
        partial_value.astype(BF).reshape(BLOCKS, small, wide), PLANE, 0, 0, tiled=True
    )
    summed = jnp.sum(got.astype(F32), axis=0).astype(BF)
    total = jnp.sum(spread(beside(summed, sparse), "zh", HIGH).astype(F32), axis=0)

    error = total[:, :wide] - target
    piece = jnp.sum(real(small) * error * error) + sparsity * jnp.sum(total[:, wide:])
    grad = (error * (2.0 * inv_batch)).astype(BF)
    grad_got = spread(beside(grad, inv_batch * piece), PLANE, BLOCKS)
    grad_got = grad_got.reshape(tokens, wide + LANES)
    part_loss = jnp.sum(grad_got[:, wide:].astype(F32))
    code_grad = jnp.dot(grad_got[:, :wide], dec_all, preferred_element_type=F32)
    code_grad = code_grad + sparsity * inv_batch * dec_norms
    pre_grad = (code_grad * slopes).astype(BF)

    loss_rows = jnp.broadcast_to(jnp.stack(pieces(part_loss))[:, None], (3, latents))
    last = jnp.concatenate([pre_grad, loss_rows, jnp.zeros((5, latents), BF)], axis=0)
    pre_here = lax.all_gather(last, "zl", axis=0)
    pre_there = swap(pre_here)

    def part_of(acts_half, pre_half):
        longer = jnp.pad(acts_half.reshape(CHIPS, tokens, chans), ((0, 0), (0, 8), (0, 0)))
        return lax.dot_general(
            longer.reshape(-1, chans),
            pre_half.reshape(-1, latents),
            (((0,), (0,)), ((), ())),
            preferred_element_type=F32,
        )

    near, far = pre_here[:, tokens:, 0].astype(F32), pre_there[:, tokens:, 0].astype(F32)
    first, second = jnp.where(core == 0, near, far), jnp.where(core == 0, far, near)
    total_loss = jnp.sum(jnp.concatenate([first, second]))
    gradient = part_of(acts_here, pre_here) + part_of(acts_there, pre_there)
    moment_new = beta_one * enc_moment + (1.0 - beta_one) * gradient
    second_new = beta_two * enc_second + (1.0 - beta_two) * gradient * gradient
    update = moment_new / first_fix / (jnp.sqrt(second_new / second_fix) + adam_eps)
    enc_new = (enc_weight.astype(F32) - learn_rate * update).astype(BF)
    return (enc_new, moment_new, second_new, total_loss)


def solution(mesh):
    fine = Mesh(mesh.devices.reshape(SIZES), NAMES)
    return jax.shard_map(
        body,
        mesh=fine,
        in_specs=(
            P(FEAT, LAYER),
            P(LAYER, FEAT),
            P(FEAT),
            P(FEAT, LAYER),
            P(LAYER),
            P(LAYER, FEAT),
            P(LAYER, FEAT),
        ),
        out_specs=(P(LAYER, FEAT), P(LAYER, FEAT), P(LAYER, FEAT), P()),
        check_vma=False,
    )
```

```python
import functools

import jax
import jax.numpy as jnp
from jax import lax
from jax.experimental import pallas as pl
from jax.experimental.pallas import tpu as pltpu
from jax.sharding import Mesh, PartitionSpec as P

D = 1792
LAYERS = 2

sparsity = 0.5
beta_one = 0.9
beta_two = 0.999
first_fix = 0.9999734386011124
second_fix = 0.0952078528862911
learn_rate = 0.002
adam_eps = 1e-08
sharpness = 4.0

SIZES = (4, 2, 4, 4, 4)
NAMES = ("zl", "core", "y", "x", "zh")
LAYER = ("zl", "core")
FEAT = ("y", "x", "zh")
PLANE = ("y", "x")
CORES = 2
CHIPS = 4
PARTS = 8
BLOCKS = 16
HIGH = 4
LANES = 128
BF = jnp.bfloat16
F32 = jnp.float32


def pieces(value, count):
    found = []
    for _ in range(count):
        top = value.astype(BF)
        found.append(top)
        value = value - top.astype(F32)
    return found


def spread(value, axes, count):
    copies = jnp.broadcast_to(value[None], (count,) + value.shape)
    return lax.all_to_all(copies, axes, 0, 0, tiled=True)


def swap(value):
    return lax.ppermute(value, "core", [(0, 1), (1, 0)])


def params(mebibytes):
    return pltpu.CompilerParams(vmem_limit_bytes=mebibytes * 1024 * 1024)


def start_blocks(source, held, sems, count):
    step = source.shape[0] // count
    found = []
    for k in range(count):
        rows = pl.ds(k * step, step)
        found.append(pltpu.make_async_copy(source.at[rows], held.at[rows], sems.at[k]))
    for copy in found:
        copy.start()
    return found


def decode_kernel(quarter_ref, bias_ref, dec_ref, out_ref, codes_ref, slopes_ref, held, sems):
    tokens = codes_ref.shape[0]
    step = held.shape[0] // CHIPS
    blocks = start_blocks(dec_ref, held, sems, CHIPS)
    sums = jnp.sum(quarter_ref[...].astype(F32), axis=0)[:tokens]
    scaled = sharpness * (sums + bias_ref[...])
    small = jnp.exp(-jnp.abs(scaled))
    soft = jnp.maximum(scaled, 0.0) + jnp.log1p(small)
    codes_ref[...] = (soft / sharpness).astype(BF)
    slopes_ref[...] = jnp.where(scaled >= 0.0, 1.0, small) / (1.0 + small)
    for k in range(CHIPS):
        blocks[k].wait()
        out_ref[:, k * step : (k + 1) * step] = lax.dot_general(
            codes_ref[...],
            held[k * step : (k + 1) * step],
            (((1,), (1,)), ((), ())),
            preferred_element_type=F32,
        ).astype(BF)


def whole():
    return pl.BlockSpec(memory_space=pltpu.VMEM)


def decode(quarter, enc_bias, dec_all, tokens):
    wide, latents = dec_all.shape
    return pl.pallas_call(
        decode_kernel,
        in_specs=[whole(), whole(), pl.BlockSpec(memory_space=pltpu.HBM)],
        out_specs=[whole(), whole(), whole()],
        out_shape=[
            jax.ShapeDtypeStruct((tokens, wide), BF),
            jax.ShapeDtypeStruct((tokens, latents), BF),
            jax.ShapeDtypeStruct((tokens, latents), F32),
        ],
        scratch_shapes=[pltpu.VMEM((wide, latents), BF), pltpu.SemaphoreType.DMA((CHIPS,))],
        compiler_params=params(50),
        cost_estimate=pl.CostEstimate(
            flops=2 * tokens * latents * wide,
            bytes_accessed=2 * wide * (latents + tokens),
            transcendentals=3 * tokens * latents,
        ),
        name="decode",
    )(quarter, enc_bias.reshape(1, latents), dec_all)


def row_sum(rows, first, last):
    row = lax.broadcasted_iota(jnp.int32, rows.shape, 0)
    return jnp.sum(jnp.where((row >= first) & (row < last), rows, 0.0), axis=0, keepdims=True)


def error_kernel(scale, got_ref, quarter_ref, mask_ref, out_ref):
    small, longer = got_ref.shape[1:]
    wide = longer - 2 * LANES
    left = wide // CHIPS - quarter_ref.shape[2]
    extra = quarter_ref[...][:, -3 * small :].astype(F32)
    target = []
    for chip in range(CHIPS):
        biases = extra[chip, 2 * small :]
        target.append(extra[chip, :small] - row_sum(biases, 0, 3))
        target.append((extra[chip, small : 2 * small] - row_sum(biases, 3, 6))[:, :left])
    total = jnp.sum(got_ref[...].astype(F32), axis=0)
    error = total[:, :wide] - jnp.concatenate(target, axis=1)
    squares = jnp.zeros((small, LANES), F32)
    for start in range(0, wide, LANES):
        part = error[:, start : start + LANES]
        squares = squares + part * part
    sparse = total[:, wide : wide + LANES] + total[:, wide + LANES :]
    lanes = scale * (mask_ref[...] * squares + sparsity * sparse)
    row = jnp.concatenate([(error * (2.0 * scale)).astype(BF), *pieces(lanes, 2)], axis=1)
    out_ref[...] = jnp.broadcast_to(row[None], out_ref.shape)


def error_copies(got, quarter, mask, scale):
    rows, longer = got.shape[1:]
    return pl.pallas_call(
        functools.partial(error_kernel, scale),
        out_shape=jax.ShapeDtypeStruct((BLOCKS, rows, longer), BF),
        compiler_params=params(16),
        cost_estimate=pl.CostEstimate(
            flops=10 * rows * longer, bytes_accessed=60 * rows * longer, transcendentals=0
        ),
        name="error",
    )(got, quarter, mask)


def back_kernel(scale, grad_ref, dec_ref, slopes_ref, norms_ref, out_ref, held, sems):
    wide, latents = held.shape
    step = wide // CHIPS
    blocks = start_blocks(dec_ref, held, sems, CHIPS)
    sums = jnp.sum(grad_ref[:, wide:].astype(F32), axis=0, keepdims=True)
    high, low = pieces(sums[:, :LANES] + sums[:, LANES:], 2)
    row = lax.broadcasted_iota(jnp.int32, (8, LANES), 0)
    both = jnp.where(row == 0, high.astype(F32), jnp.where(row == 1, low.astype(F32), 0.0))
    block = jnp.concatenate([both, jnp.zeros((8, latents - LANES), F32)], axis=1)
    code_grad = sparsity * scale * norms_ref[...]
    for k in range(CHIPS):
        blocks[k].wait()
        code_grad = code_grad + jnp.dot(
            grad_ref[:, k * step : (k + 1) * step],
            held[k * step : (k + 1) * step],
            preferred_element_type=F32,
        )
    out_ref[...] = jnp.concatenate([code_grad * slopes_ref[...], block], axis=0).astype(BF)


def back(grads, dec_all, slopes, norms, scale):
    tokens = grads.shape[0]
    wide, latents = dec_all.shape
    return pl.pallas_call(
        functools.partial(back_kernel, scale),
        in_specs=[whole(), pl.BlockSpec(memory_space=pltpu.HBM), whole(), whole()],
        out_specs=whole(),
        out_shape=jax.ShapeDtypeStruct((tokens + 8, latents), BF),
        scratch_shapes=[pltpu.VMEM((wide, latents), BF), pltpu.SemaphoreType.DMA((CHIPS,))],
        compiler_params=params(50),
        cost_estimate=pl.CostEstimate(
            flops=2 * tokens * latents * wide,
            bytes_accessed=2 * wide * (latents + tokens),
            transcendentals=0,
        ),
        name="back",
    )(grads, dec_all, slopes, norms.reshape(1, latents))


def body(acts, enc_weight, enc_bias, dec_weight, dec_bias, enc_moment, enc_second):
    rows, chans = acts.shape
    latents = enc_weight.shape[1]
    inv_batch = 1.0 / (rows * BLOCKS * HIGH)
    wide = PARTS * chans
    core = lax.axis_index("core")
    chip = lax.axis_index("zl")
    share = (rows + 1) // PARTS
    half = CHIPS * share
    small = HIGH * share
    tokens = BLOCKS * small

    dec_all = lax.all_gather(dec_weight.T, LAYER, axis=0, tiled=True)
    enc_there = swap(enc_weight)
    bias_there = swap(dec_bias)

    def ordered(near, far, axis):
        first, second = jnp.where(core == 0, near, far), jnp.where(core == 0, far, near)
        return jnp.concatenate([first, second], axis=axis)

    padded = jnp.concatenate([acts, jnp.zeros((1, chans), BF)], axis=0)
    low, high = padded[:half], padded[half:]
    taken = swap(jnp.where(core == 0, high, low))
    pair = ordered(jnp.where(core == 0, low, high), taken, 1)
    column = spread(pair, "zh", HIGH).reshape(HIGH, CHIPS, share, 2 * chans)
    column = column.transpose(1, 0, 2, 3).reshape(CHIPS, small, 2 * chans)
    gathered = spread(column, PLANE, BLOCKS).transpose(1, 0, 2, 3)
    gathered = gathered.reshape(CHIPS * tokens, 2 * chans)
    first_half, second_half = gathered[:, :chans], gathered[:, chans:]
    acts_here = jnp.where(core == 0, first_half, second_half)
    acts_there = swap(jnp.where(core == 0, second_half, first_half))

    enc_pair = ordered(enc_weight, enc_there, 0)
    sums = jnp.dot(gathered, enc_pair, preferred_element_type=F32).astype(BF)

    def folded(rows_of):
        fill = [(0, 0)] * (rows_of.ndim - 1) + [(0, 2 * latents - 2 * chans)]
        rest = jnp.pad(rows_of[..., latents:], fill)
        return jnp.concatenate([rows_of[..., :latents], rest], axis=-2)

    bias_rows = folded(jnp.stack(pieces(ordered(dec_bias, bias_there, 0), 3)))
    bias_rows = jnp.pad(bias_rows, ((0, small - 6), (0, 0)))
    bias_rows = jnp.broadcast_to(bias_rows[None], (CHIPS, small, latents))
    extra = jnp.concatenate([folded(column), bias_rows], axis=1)
    sending = jnp.concatenate([sums.reshape(CHIPS, tokens, latents), extra], axis=1)
    quarter = lax.all_to_all(sending, "zl", 0, 0, tiled=True)
    partial_value, codes, slopes = decode(quarter, enc_bias, dec_all, tokens)

    dec_norms = jnp.zeros((latents,), F32)
    for layer in range(LAYERS):
        block = dec_all[layer * (wide // LAYERS) : (layer + 1) * (wide // LAYERS)].astype(F32)
        dec_norms = dec_norms + jnp.sqrt(jnp.sum(block * block, axis=0))

    place = lax.broadcasted_iota(jnp.int32, (small, LANES), 0) % share
    real = (core * half + chip * share + place < rows).astype(F32)
    weighed = jnp.sum((codes.astype(F32) * dec_norms).reshape(BLOCKS, small, latents), axis=0)
    sparse = real * sum(weighed[:, k : k + LANES] for k in range(0, latents, LANES))

    got = lax.all_to_all(
        partial_value.reshape(BLOCKS, small, wide), PLANE, 0, 0, tiled=True
    )
    summed = jnp.sum(got.astype(F32), axis=0).astype(BF)
    again = spread(jnp.concatenate([summed, *pieces(sparse, 2)], axis=1), "zh", HIGH)
    again, acts_there = lax.optimization_barrier((again, acts_there))
    copies = error_copies(again, quarter, real, inv_batch)
    grads = lax.all_to_all(copies, PLANE, 0, 0, tiled=True)
    last = back(grads.reshape(tokens, wide + 2 * LANES), dec_all, slopes, dec_norms, inv_batch)
    pre_here = lax.all_gather(last, "zl", axis=0)
    pre_there = swap(pre_here)

    def part_of(acts_half, pre_half):
        longer = jnp.pad(acts_half.reshape(CHIPS, tokens, chans), ((0, 0), (0, 8), (0, 0)))
        return lax.dot_general(
            longer.reshape(-1, chans),
            pre_half.reshape(-1, latents),
            (((0,), (0,)), ((), ())),
            preferred_element_type=F32,
        )

    near = pre_here[:, tokens : tokens + 2, :LANES].astype(F32)
    far = pre_there[:, tokens : tokens + 2, :LANES].astype(F32)
    first, second = jnp.where(core == 0, near, far), jnp.where(core == 0, far, near)
    total_loss = jnp.sum(first + second)
    gradient = part_of(acts_here, pre_here) + part_of(acts_there, pre_there)
    moment_new = beta_one * enc_moment + (1.0 - beta_one) * gradient
    second_new = beta_two * enc_second + (1.0 - beta_two) * gradient * gradient
    update = moment_new / first_fix / (jnp.sqrt(second_new / second_fix) + adam_eps)
    enc_new = (enc_weight.astype(F32) - learn_rate * update).astype(BF)
    return (enc_new, moment_new, second_new, total_loss)


def solution(mesh):
    fine = Mesh(mesh.devices.reshape(SIZES), NAMES)
    return jax.shard_map(
        body,
        mesh=fine,
        in_specs=(
            P(FEAT, LAYER),
            P(LAYER, FEAT),
            P(FEAT),
            P(FEAT, LAYER),
            P(LAYER),
            P(LAYER, FEAT),
            P(LAYER, FEAT),
        ),
        out_specs=(P(LAYER, FEAT), P(LAYER, FEAT), P(LAYER, FEAT), P()),
        check_vma=False,
    )
```

```python
import functools

import jax
import jax.numpy as jnp
from jax import lax
from jax.experimental import pallas as pl
from jax.experimental.pallas import tpu as pltpu
from jax.sharding import Mesh, PartitionSpec as P

D = 1792
LAYERS = 2

sparsity = 0.5
beta_one = 0.9
beta_two = 0.999
first_fix = 0.9999734386011124
second_fix = 0.0952078528862911
learn_rate = 0.002
adam_eps = 1e-08
sharpness = 4.0

SIZES = (4, 2, 4, 4, 4)
NAMES = ("zl", "core", "y", "x", "zh")
LAYER = ("zl", "core")
FEAT = ("y", "x", "zh")
PLANE = ("y", "x")
CORES = 2
CHIPS = 4
PARTS = 8
BLOCKS = 16
HIGH = 4
LANES = 128
BF = jnp.bfloat16
F32 = jnp.float32


def pieces(value, count):
    found = []
    for _ in range(count):
        top = value.astype(BF)
        found.append(top)
        value = value - top.astype(F32)
    return found


def spread(value, axes, count):
    copies = jnp.broadcast_to(value[None], (count,) + value.shape)
    return lax.all_to_all(copies, axes, 0, 0, tiled=True)


def swap(value):
    return lax.ppermute(value, "core", [(0, 1), (1, 0)])


def params(mebibytes):
    return pltpu.CompilerParams(vmem_limit_bytes=mebibytes * 1024 * 1024)


def start_blocks(source, held, sems, count):
    step = source.shape[0] // count
    found = []
    for k in range(count):
        rows = pl.ds(k * step, step)
        found.append(pltpu.make_async_copy(source.at[rows], held.at[rows], sems.at[k]))
    for copy in found:
        copy.start()
    return found


def decode_kernel(quarter_ref, bias_ref, dec_ref, out_ref, codes_ref, slopes_ref, held, sems):
    step = held.shape[0] // CHIPS
    blocks = start_blocks(dec_ref, held, sems, CHIPS)
    sums = jnp.sum(quarter_ref[...].astype(F32), axis=0)
    scaled = sharpness * (sums + bias_ref[...])
    small = jnp.exp(-jnp.abs(scaled))
    soft = jnp.maximum(scaled, 0.0) + jnp.log1p(small)
    codes_ref[...] = (soft / sharpness).astype(BF)
    slopes_ref[...] = jnp.where(scaled >= 0.0, 1.0, small) / (1.0 + small)
    for k in range(CHIPS):
        blocks[k].wait()
        out_ref[:, k * step : (k + 1) * step] = lax.dot_general(
            codes_ref[...],
            held[k * step : (k + 1) * step],
            (((1,), (1,)), ((), ())),
            preferred_element_type=F32,
        ).astype(BF)


def whole():
    return pl.BlockSpec(memory_space=pltpu.VMEM)


def decode(quarter, enc_bias, dec_all, tokens):
    wide, latents = dec_all.shape
    return pl.pallas_call(
        decode_kernel,
        in_specs=[whole(), whole(), pl.BlockSpec(memory_space=pltpu.HBM)],
        out_specs=[whole(), whole(), whole()],
        out_shape=[
            jax.ShapeDtypeStruct((tokens, wide), BF),
            jax.ShapeDtypeStruct((tokens, latents), BF),
            jax.ShapeDtypeStruct((tokens, latents), F32),
        ],
        scratch_shapes=[pltpu.VMEM((wide, latents), BF), pltpu.SemaphoreType.DMA((CHIPS,))],
        compiler_params=params(50),
        cost_estimate=pl.CostEstimate(
            flops=2 * tokens * latents * wide,
            bytes_accessed=2 * wide * (latents + tokens),
            transcendentals=3 * tokens * latents,
        ),
        name="decode",
    )(quarter, enc_bias.reshape(1, latents), dec_all)


def row_sum(rows, first, last):
    row = lax.broadcasted_iota(jnp.int32, rows.shape, 0)
    return jnp.sum(jnp.where((row >= first) & (row < last), rows, 0.0), axis=0, keepdims=True)


def error_kernel(scale, got_ref, extra_ref, mask_ref, out_ref):
    small, longer = got_ref.shape[1:]
    wide = longer - LANES
    left = wide // CHIPS - extra_ref.shape[2]
    extra = extra_ref[...].astype(F32)
    target = []
    for chip in range(CHIPS):
        biases = extra[chip, 2 * small :]
        target.append(extra[chip, :small] - row_sum(biases, 0, 3))
        target.append((extra[chip, small : 2 * small] - row_sum(biases, 3, 6))[:, :left])
    total = jnp.sum(got_ref[...].astype(F32), axis=0)
    error = total[:, :wide] - jnp.concatenate(target, axis=1)
    squares = jnp.zeros((small, LANES), F32)
    for start in range(0, wide, LANES):
        part = error[:, start : start + LANES]
        squares = squares + part * part
    lanes = scale * (mask_ref[...] * squares + sparsity * total[:, wide:])
    row = jnp.concatenate([error * (2.0 * scale), lanes], axis=1).astype(BF)
    out_ref[...] = jnp.broadcast_to(row[None], out_ref.shape)


def error_copies(got, extra, mask, scale):
    rows, longer = got.shape[1:]
    return pl.pallas_call(
        functools.partial(error_kernel, scale),
        out_shape=jax.ShapeDtypeStruct((BLOCKS, rows, longer), BF),
        compiler_params=params(16),
        cost_estimate=pl.CostEstimate(
            flops=10 * rows * longer, bytes_accessed=60 * rows * longer, transcendentals=0
        ),
        name="error",
    )(got, extra, mask)


def back_kernel(scale, grad_ref, dec_ref, slopes_ref, norms_ref, out_ref, held, sems):
    wide, latents = held.shape
    step = wide // CHIPS
    blocks = start_blocks(dec_ref, held, sems, CHIPS)
    sums = jnp.sum(grad_ref[:, wide:].astype(F32), axis=0, keepdims=True)
    high, low = pieces(sums, 2)
    row = lax.broadcasted_iota(jnp.int32, (8, LANES), 0)
    both = jnp.where(row == 0, high.astype(F32), jnp.where(row == 1, low.astype(F32), 0.0))
    block = jnp.concatenate([both, jnp.zeros((8, latents - LANES), F32)], axis=1)
    code_grad = sparsity * scale * norms_ref[...]
    for k in range(CHIPS):
        blocks[k].wait()
        code_grad = code_grad + jnp.dot(
            grad_ref[:, k * step : (k + 1) * step],
            held[k * step : (k + 1) * step],
            preferred_element_type=F32,
        )
    out_ref[...] = jnp.concatenate([code_grad * slopes_ref[...], block], axis=0).astype(BF)


def back(grads, dec_all, slopes, norms, scale):
    tokens = grads.shape[0]
    wide, latents = dec_all.shape
    return pl.pallas_call(
        functools.partial(back_kernel, scale),
        in_specs=[whole(), pl.BlockSpec(memory_space=pltpu.HBM), whole(), whole()],
        out_specs=whole(),
        out_shape=jax.ShapeDtypeStruct((tokens + 8, latents), BF),
        scratch_shapes=[pltpu.VMEM((wide, latents), BF), pltpu.SemaphoreType.DMA((CHIPS,))],
        compiler_params=params(50),
        cost_estimate=pl.CostEstimate(
            flops=2 * tokens * latents * wide,
            bytes_accessed=2 * wide * (latents + tokens),
            transcendentals=0,
        ),
        name="back",
    )(grads, dec_all, slopes, norms.reshape(1, latents))


def body(acts, enc_weight, enc_bias, dec_weight, dec_bias, enc_moment, enc_second):
    rows, chans = acts.shape
    latents = enc_weight.shape[1]
    inv_batch = 1.0 / (rows * BLOCKS * HIGH)
    wide = PARTS * chans
    core = lax.axis_index("core")
    chip = lax.axis_index("zl")
    share = (rows + 1) // PARTS
    half = CHIPS * share
    small = HIGH * share
    tokens = BLOCKS * small

    dec_all = lax.all_gather(dec_weight.T, LAYER, axis=0, tiled=True)
    enc_there = swap(enc_weight)
    bias_there = swap(dec_bias)

    def ordered(near, far, axis):
        first, second = jnp.where(core == 0, near, far), jnp.where(core == 0, far, near)
        return jnp.concatenate([first, second], axis=axis)

    padded = jnp.concatenate([acts, jnp.zeros((1, chans), BF)], axis=0)
    halves = jnp.broadcast_to(padded.reshape(CORES, 1, half, chans), (CORES, HIGH, half, chans))
    halves = halves.reshape(CORES * HIGH, half, chans)
    column = lax.all_to_all(halves, ("core", "zh"), 0, 0, tiled=True)
    column = column.reshape(CORES, HIGH, CHIPS, share, chans).transpose(2, 1, 3, 0, 4)
    column = column.reshape(CHIPS, small, 2 * chans)
    gathered = spread(column, PLANE, BLOCKS).transpose(1, 0, 2, 3)
    gathered = gathered.reshape(CHIPS * tokens, 2 * chans)

    def folded(rows_of):
        fill = [(0, 0)] * (rows_of.ndim - 1) + [(0, 2 * latents - 2 * chans)]
        rest = jnp.pad(rows_of[..., latents:], fill)
        return jnp.concatenate([rows_of[..., :latents], rest], axis=-2)

    bias_rows = folded(jnp.stack(pieces(ordered(dec_bias, bias_there, 0), 3)))
    bias_rows = jnp.pad(bias_rows, ((0, small - 6), (0, 0)))
    bias_rows = jnp.broadcast_to(bias_rows[None], (CHIPS, small, latents))
    extra = jnp.concatenate([folded(column), bias_rows], axis=1)
    came = []
    for away in range(CHIPS):
        block = lax.dynamic_index_in_dim(extra, (chip + away) & (CHIPS - 1), 0)
        ways = [(i, (i + away) % CHIPS) for i in range(CHIPS)]
        came.append(lax.ppermute(block, "zl", ways) if away else block)
    gathered, *came = lax.optimization_barrier((gathered, *came))
    turned = jnp.concatenate([came[-k % CHIPS] for k in range(2 * CHIPS - 1)], axis=0)
    mine = lax.dynamic_slice_in_dim(turned, (CHIPS - chip) & (CHIPS - 1), CHIPS, axis=0)

    first_half, second_half = gathered[:, :chans], gathered[:, chans:]
    acts_here = jnp.where(core == 0, first_half, second_half)
    acts_there = swap(jnp.where(core == 0, second_half, first_half))

    enc_pair = ordered(enc_weight, enc_there, 0)
    sums = jnp.dot(gathered, enc_pair, preferred_element_type=F32).astype(BF)
    quarter = lax.all_to_all(sums.reshape(CHIPS, tokens, latents), "zl", 0, 0, tiled=True)
    partial_value, codes, slopes = decode(quarter, enc_bias, dec_all, tokens)

    dec_norms = jnp.zeros((latents,), F32)
    for layer in range(LAYERS):
        block = dec_all[layer * (wide // LAYERS) : (layer + 1) * (wide // LAYERS)].astype(F32)
        dec_norms = dec_norms + jnp.sqrt(jnp.sum(block * block, axis=0))

    place = lax.broadcasted_iota(jnp.int32, (small, LANES), 0) & (share - 1)
    real = (core * half + chip * share + place < rows).astype(F32)
    weighed = jnp.sum((codes.astype(F32) * dec_norms).reshape(BLOCKS, small, latents), axis=0)
    sparse = real * sum(weighed[:, k : k + LANES] for k in range(0, latents, LANES))

    got = lax.all_to_all(
        partial_value.reshape(BLOCKS, small, wide), PLANE, 0, 0, tiled=True
    )
    summed = jnp.sum(got.astype(F32), axis=0).astype(BF)
    again = spread(jnp.concatenate([summed, sparse.astype(BF)], axis=1), "zh", HIGH)
    again, acts_there = lax.optimization_barrier((again, acts_there))
    copies = error_copies(again, mine, real, inv_batch)
    grads = lax.all_to_all(copies, PLANE, 0, 0, tiled=True)
    last = back(grads.reshape(tokens, wide + LANES), dec_all, slopes, dec_norms, inv_batch)
    pre_here = lax.all_gather(last, "zl", axis=0)
    pre_there = swap(pre_here)

    def part_of(acts_half, pre_half):
        longer = jnp.pad(acts_half.reshape(CHIPS, tokens, chans), ((0, 0), (0, 8), (0, 0)))
        return lax.dot_general(
            longer.reshape(-1, chans),
            pre_half.reshape(-1, latents),
            (((0,), (0,)), ((), ())),
            preferred_element_type=F32,
        )

    near = pre_here[:, tokens : tokens + 2, :LANES].astype(F32)
    far = pre_there[:, tokens : tokens + 2, :LANES].astype(F32)
    first, second = jnp.where(core == 0, near, far), jnp.where(core == 0, far, near)
    total_loss = jnp.sum(first + second)
    gradient = part_of(acts_here, pre_here) + part_of(acts_there, pre_there)
    moment_new = beta_one * enc_moment + (1.0 - beta_one) * gradient
    second_new = beta_two * enc_second + (1.0 - beta_two) * gradient * gradient
    update = moment_new / first_fix / (jnp.sqrt(second_new / second_fix) + adam_eps)
    enc_new = (enc_weight.astype(F32) - learn_rate * update).astype(BF)
    return (enc_new, moment_new, second_new, total_loss)


def solution(mesh):
    fine = Mesh(mesh.devices.reshape(SIZES), NAMES)
    return jax.shard_map(
        body,
        mesh=fine,
        in_specs=(
            P(FEAT, LAYER),
            P(LAYER, FEAT),
            P(FEAT),
            P(FEAT, LAYER),
            P(LAYER),
            P(LAYER, FEAT),
            P(LAYER, FEAT),
        ),
        out_specs=(P(LAYER, FEAT), P(LAYER, FEAT), P(LAYER, FEAT), P()),
        check_vma=False,
    )
```

```python
import functools

import jax
import jax.numpy as jnp
from jax import lax
from jax.experimental import pallas as pl
from jax.experimental.pallas import tpu as pltpu
from jax.sharding import Mesh, PartitionSpec as P

D = 1792
LAYERS = 2

sparsity = 0.5
beta_one = 0.9
beta_two = 0.999
first_fix = 0.9999734386011124
second_fix = 0.0952078528862911
learn_rate = 0.002
adam_eps = 1e-08
sharpness = 4.0

SIZES = (4, 2, 4, 4, 4)
NAMES = ("zl", "core", "y", "x", "zh")
LAYER = ("zl", "core")
FEAT = ("y", "x", "zh")
PLANE = ("y", "x")
CORES = 2
CHIPS = 4
PARTS = 8
BLOCKS = 16
HIGH = 4
LANES = 128
BF = jnp.bfloat16
F32 = jnp.float32


def pieces(value, count):
    found = []
    for _ in range(count):
        top = value.astype(BF)
        found.append(top)
        value = value - top.astype(F32)
    return found


def spread(value, axes, count):
    copies = jnp.broadcast_to(value[None], (count,) + value.shape)
    return lax.all_to_all(copies, axes, 0, 0, tiled=True)


def swap(value):
    return lax.ppermute(value, "core", [(0, 1), (1, 0)])


def params(mebibytes):
    return pltpu.CompilerParams(vmem_limit_bytes=mebibytes * 1024 * 1024)


def start_blocks(sources, held, sems):
    step = sources[0].shape[0] // CHIPS
    found = []
    for chip in range(CHIPS):
        for k, source in enumerate(sources):
            place = chip * len(sources) + k
            rows, there = pl.ds(chip * step, step), pl.ds(place * step, step)
            found.append(pltpu.make_async_copy(source.at[rows], held.at[there], sems.at[place]))
    for copy in found:
        copy.start()
    return found


def await_chip(blocks, chip):
    for copy in blocks[chip * CORES : (chip + 1) * CORES]:
        copy.wait()


def decode_kernel(
    quarter_ref, bias_ref, here_ref, there_ref, out_ref, codes_ref, slopes_ref, held, sems
):
    step = held.shape[0] // CHIPS
    blocks = start_blocks((here_ref, there_ref), held, sems)
    sums = jnp.sum(quarter_ref[...].astype(F32), axis=0)
    scaled = sharpness * (sums + bias_ref[...])
    small = jnp.exp(-jnp.abs(scaled))
    soft = jnp.maximum(scaled, 0.0) + jnp.log1p(small)
    codes_ref[...] = (soft / sharpness).astype(BF)
    slopes_ref[...] = jnp.where(scaled >= 0.0, 1.0, small) / (1.0 + small)
    for k in range(CHIPS):
        await_chip(blocks, k)
        out_ref[:, k * step : (k + 1) * step] = lax.dot_general(
            codes_ref[...],
            held[k * step : (k + 1) * step],
            (((1,), (1,)), ((), ())),
            preferred_element_type=F32,
        ).astype(BF)


def in_hbm():
    return pl.BlockSpec(memory_space=pltpu.HBM)


def whole():
    return pl.BlockSpec(memory_space=pltpu.VMEM)


def decode(quarter, enc_bias, dec_here, dec_there, tokens):
    wide, latents = CORES * dec_here.shape[0], dec_here.shape[1]
    return pl.pallas_call(
        decode_kernel,
        in_specs=[whole(), whole(), in_hbm(), in_hbm()],
        out_specs=[whole(), whole(), whole()],
        out_shape=[
            jax.ShapeDtypeStruct((tokens, wide), BF),
            jax.ShapeDtypeStruct((tokens, latents), BF),
            jax.ShapeDtypeStruct((tokens, latents), F32),
        ],
        scratch_shapes=[pltpu.VMEM((wide, latents), BF), pltpu.SemaphoreType.DMA((PARTS,))],
        compiler_params=params(50),
        cost_estimate=pl.CostEstimate(
            flops=2 * tokens * latents * wide,
            bytes_accessed=2 * wide * (latents + tokens),
            transcendentals=3 * tokens * latents,
        ),
        name="decode",
    )(quarter, enc_bias.reshape(1, latents), dec_here, dec_there)


def row_sum(rows, first, last):
    row = lax.broadcasted_iota(jnp.int32, rows.shape, 0)
    return jnp.sum(jnp.where((row >= first) & (row < last), rows, 0.0), axis=0, keepdims=True)


def error_kernel(scale, got_ref, extra_ref, mask_ref, out_ref):
    small, longer = got_ref.shape[1:]
    wide = longer - LANES
    left = wide // CHIPS - extra_ref.shape[2]
    extra = extra_ref[...].astype(F32)
    target = []
    for chip in range(CHIPS):
        biases = extra[chip, 2 * small :]
        target.append(extra[chip, :small] - row_sum(biases, 0, 3))
        target.append((extra[chip, small : 2 * small] - row_sum(biases, 3, 6))[:, :left])
    total = jnp.sum(got_ref[...].astype(F32), axis=0)
    error = total[:, :wide] - jnp.concatenate(target, axis=1)
    squares = jnp.zeros((small, LANES), F32)
    for start in range(0, wide, LANES):
        part = error[:, start : start + LANES]
        squares = squares + part * part
    lanes = scale * (mask_ref[...] * squares + sparsity * total[:, wide:])
    row = jnp.concatenate([error * (2.0 * scale), lanes], axis=1).astype(BF)
    out_ref[...] = jnp.broadcast_to(row[None], out_ref.shape)


def error_copies(got, extra, mask, scale):
    rows, longer = got.shape[1:]
    return pl.pallas_call(
        functools.partial(error_kernel, scale),
        out_shape=jax.ShapeDtypeStruct((BLOCKS, rows, longer), BF),
        compiler_params=params(16),
        cost_estimate=pl.CostEstimate(
            flops=10 * rows * longer, bytes_accessed=60 * rows * longer, transcendentals=0
        ),
        name="error",
    )(got, extra, mask)


def back_kernel(
    scale, grad_ref, here_ref, there_ref, slopes_ref, norms_ref, out_ref, held, sems
):
    wide, latents = held.shape
    step = wide // CHIPS
    blocks = start_blocks((here_ref, there_ref), held, sems)
    sums = jnp.sum(grad_ref[:, wide:].astype(F32), axis=0, keepdims=True)
    high, low = pieces(sums, 2)
    row = lax.broadcasted_iota(jnp.int32, (8, LANES), 0)
    both = jnp.where(row == 0, high.astype(F32), jnp.where(row == 1, low.astype(F32), 0.0))
    block = jnp.concatenate([both, jnp.zeros((8, latents - LANES), F32)], axis=1)
    code_grad = sparsity * scale * norms_ref[...]
    for k in range(CHIPS):
        await_chip(blocks, k)
        code_grad = code_grad + jnp.dot(
            grad_ref[:, k * step : (k + 1) * step],
            held[k * step : (k + 1) * step],
            preferred_element_type=F32,
        )
    out_ref[...] = jnp.concatenate([code_grad * slopes_ref[...], block], axis=0).astype(BF)


def back(grads, dec_here, dec_there, slopes, norms, scale):
    tokens = grads.shape[0]
    wide, latents = CORES * dec_here.shape[0], dec_here.shape[1]
    return pl.pallas_call(
        functools.partial(back_kernel, scale),
        in_specs=[whole(), in_hbm(), in_hbm(), whole(), whole()],
        out_specs=whole(),
        out_shape=jax.ShapeDtypeStruct((tokens + 8, latents), BF),
        scratch_shapes=[pltpu.VMEM((wide, latents), BF), pltpu.SemaphoreType.DMA((PARTS,))],
        compiler_params=params(50),
        cost_estimate=pl.CostEstimate(
            flops=2 * tokens * latents * wide,
            bytes_accessed=2 * wide * (latents + tokens),
            transcendentals=0,
        ),
        name="back",
    )(grads, dec_here, dec_there, slopes, norms.reshape(1, latents))


def body(acts, enc_weight, enc_bias, dec_weight, dec_bias, enc_moment, enc_second):
    rows, chans = acts.shape
    latents = enc_weight.shape[1]
    inv_batch = 1.0 / (rows * BLOCKS * HIGH)
    wide = PARTS * chans
    core = lax.axis_index("core")
    chip = lax.axis_index("zl")
    share = (rows + 1) // PARTS
    half = CHIPS * share
    small = HIGH * share
    tokens = BLOCKS * small

    dec_here = lax.all_gather(dec_weight.T, "zl", axis=0, tiled=True)
    dec_there = swap(dec_here)
    enc_there = swap(enc_weight)
    bias_there = swap(dec_bias)

    padded = jnp.concatenate([acts, jnp.zeros((1, chans), BF)], axis=0)
    halves = jnp.broadcast_to(padded.reshape(CORES, 1, half, chans), (CORES, HIGH, half, chans))
    halves = halves.reshape(CORES * HIGH, half, chans)
    column = lax.all_to_all(halves, ("core", "zh"), 0, 0, tiled=True)
    column = column.reshape(CORES, HIGH, CHIPS, share, chans)
    column = jnp.where(core == 0, column, column[::-1])
    column = column.transpose(2, 1, 3, 0, 4)
    column = column.reshape(CHIPS, small, 2 * chans)
    gathered = spread(column, PLANE, BLOCKS).transpose(1, 0, 2, 3)
    gathered = gathered.reshape(CHIPS * tokens, 2 * chans)

    def folded(rows_of):
        fill = [(0, 0)] * (rows_of.ndim - 1) + [(0, 2 * latents - 2 * chans)]
        rest = jnp.pad(rows_of[..., latents:], fill)
        return jnp.concatenate([rows_of[..., :latents], rest], axis=-2)

    bias_rows = folded(jnp.stack(pieces(jnp.concatenate([dec_bias, bias_there]), 3)))
    bias_rows = jnp.pad(bias_rows, ((0, small - 6), (0, 0)))
    bias_rows = jnp.broadcast_to(bias_rows[None], (CHIPS, small, latents))
    extra = jnp.concatenate([folded(column), bias_rows], axis=1)
    came = []
    for away in range(CHIPS):
        block = lax.dynamic_index_in_dim(extra, (chip + away) & (CHIPS - 1), 0)
        ways = [(i, (i + away) % CHIPS) for i in range(CHIPS)]
        came.append(lax.ppermute(block, "zl", ways) if away else block)
    gathered, *came = lax.optimization_barrier((gathered, *came))
    turned = jnp.concatenate([came[-k % CHIPS] for k in range(2 * CHIPS - 1)], axis=0)
    mine = lax.dynamic_slice_in_dim(turned, (CHIPS - chip) & (CHIPS - 1), CHIPS, axis=0)

    acts_here = gathered[:, :chans]
    acts_there = swap(gathered[:, chans:])
    enc_pair = jnp.concatenate([enc_weight, enc_there], axis=0)
    sums = jnp.dot(gathered, enc_pair, preferred_element_type=F32).astype(BF)
    quarter = lax.all_to_all(sums.reshape(CHIPS, tokens, latents), "zl", 0, 0, tiled=True)
    partial_value, codes, slopes = decode(quarter, enc_bias, dec_here, dec_there, tokens)

    dec_norms = jnp.zeros((latents,), F32)
    for layer in range(LAYERS):
        rows_of = slice(layer * CHIPS // LAYERS * chans, (layer + 1) * CHIPS // LAYERS * chans)
        near, far = dec_here[rows_of].astype(F32), dec_there[rows_of].astype(F32)
        dec_norms = dec_norms + jnp.sqrt(jnp.sum(near * near + far * far, axis=0))

    place = lax.broadcasted_iota(jnp.int32, (small, LANES), 0) & (share - 1)
    real = (core * half + chip * share + place < rows).astype(F32)
    weighed = jnp.sum((codes.astype(F32) * dec_norms).reshape(BLOCKS, small, latents), axis=0)
    sparse = real * sum(weighed[:, k : k + LANES] for k in range(0, latents, LANES))

    got = lax.all_to_all(
        partial_value.reshape(BLOCKS, small, wide), PLANE, 0, 0, tiled=True
    )
    summed = jnp.sum(got.astype(F32), axis=0).astype(BF)
    again = lax.all_gather(jnp.concatenate([summed, sparse.astype(BF)], axis=1), "zh", axis=0)
    again, acts_there = lax.optimization_barrier((again, acts_there))
    copies = error_copies(again, mine, real, inv_batch)
    grads = lax.all_to_all(copies, PLANE, 0, 0, tiled=True)
    last = back(grads.reshape(tokens, wide + LANES), dec_here, dec_there, slopes, dec_norms, inv_batch)
    pre_here = lax.all_gather(last, "zl", axis=0)
    pre_there = swap(pre_here)

    def part_of(acts_half, pre_half):
        longer = jnp.pad(acts_half.reshape(CHIPS, tokens, chans), ((0, 0), (0, 8), (0, 0)))
        return lax.dot_general(
            longer.reshape(-1, chans),
            pre_half.reshape(-1, latents),
            (((0,), (0,)), ((), ())),
            preferred_element_type=F32,
        )

    near = pre_here[:, tokens : tokens + 2, :LANES].astype(F32)
    far = pre_there[:, tokens : tokens + 2, :LANES].astype(F32)
    first, second = jnp.where(core == 0, near, far), jnp.where(core == 0, far, near)
    total_loss = jnp.sum(first + second)
    gradient = part_of(acts_here, pre_here) + part_of(acts_there, pre_there)
    moment_new = beta_one * enc_moment + (1.0 - beta_one) * gradient
    second_new = beta_two * enc_second + (1.0 - beta_two) * gradient * gradient
    update = moment_new / first_fix / (jnp.sqrt(second_new / second_fix) + adam_eps)
    enc_new = (enc_weight.astype(F32) - learn_rate * update).astype(BF)
    return (enc_new, moment_new, second_new, total_loss)


def solution(mesh):
    fine = Mesh(mesh.devices.reshape(SIZES), NAMES)
    return jax.shard_map(
        body,
        mesh=fine,
        in_specs=(
            P(FEAT, LAYER),
            P(LAYER, FEAT),
            P(FEAT),
            P(FEAT, LAYER),
            P(LAYER),
            P(LAYER, FEAT),
            P(LAYER, FEAT),
        ),
        out_specs=(P(LAYER, FEAT), P(LAYER, FEAT), P(LAYER, FEAT), P()),
        check_vma=False,
    )
```

```python
import functools

import jax
import jax.numpy as jnp
from jax import lax
from jax.experimental import pallas as pl
from jax.experimental.pallas import tpu as pltpu
from jax.sharding import Mesh, PartitionSpec as P

D = 1792
LAYERS = 2

sparsity = 0.5
beta_one = 0.9
beta_two = 0.999
first_fix = 0.9999734386011124
second_fix = 0.0952078528862911
learn_rate = 0.002
adam_eps = 1e-08
sharpness = 4.0

SIZES = (4, 2, 4, 4, 4)
NAMES = ("zl", "core", "y", "x", "zh")
LAYER = ("zl", "core")
FEAT = ("y", "x", "zh")
PLANE = ("y", "x")
CORES = 2
CHIPS = 4
PARTS = 8
BLOCKS = 16
HIGH = 4
LANES = 128
BF = jnp.bfloat16
F32 = jnp.float32


def pieces(value, count):
    found = []
    for _ in range(count):
        top = value.astype(BF)
        found.append(top)
        value = value - top.astype(F32)
    return found


def spread(value, axes, count):
    copies = jnp.broadcast_to(value[None], (count,) + value.shape)
    return lax.all_to_all(copies, axes, 0, 0, tiled=True)


def swap(value):
    return lax.ppermute(value, "core", [(0, 1), (1, 0)])


def params(mebibytes):
    return pltpu.CompilerParams(vmem_limit_bytes=mebibytes * 1024 * 1024)


def start_blocks(sources, held, sems):
    step = sources[0].shape[0]
    found = []
    for place, source in enumerate(sources):
        first = step if source.shape[0] > step else 0
        there = pl.ds(place * step, step)
        found.append(
            pltpu.make_async_copy(source.at[pl.ds(first, step)], held.at[there], sems.at[place])
        )
    for copy in found:
        copy.start()
    return found


def await_chip(blocks, chip):
    for copy in blocks[chip * CORES : (chip + 1) * CORES]:
        copy.wait()


def decode_kernel(quarter_ref, bias_ref, *refs):
    *dec_refs, out_ref, codes_ref, slopes_ref, held, sems = refs
    step = held.shape[0] // CHIPS
    blocks = start_blocks(dec_refs, held, sems)
    sums = jnp.sum(quarter_ref[...].astype(F32), axis=0)
    scaled = sharpness * (sums + bias_ref[...])
    small = jnp.exp(-jnp.abs(scaled))
    soft = jnp.maximum(scaled, 0.0) + jnp.log1p(small)
    codes_ref[...] = (soft / sharpness).astype(BF)
    slopes_ref[...] = jnp.where(scaled >= 0.0, 1.0, small) / (1.0 + small)
    for k in range(CHIPS):
        await_chip(blocks, k)
        out_ref[:, k * step : (k + 1) * step] = lax.dot_general(
            codes_ref[...],
            held[k * step : (k + 1) * step],
            (((1,), (1,)), ((), ())),
            preferred_element_type=F32,
        ).astype(BF)


def in_hbm():
    return pl.BlockSpec(memory_space=pltpu.HBM)


def whole():
    return pl.BlockSpec(memory_space=pltpu.VMEM)


def decode(quarter, enc_bias, dec_blocks, tokens):
    wide, latents = PARTS * dec_blocks[0].shape[0], dec_blocks[0].shape[1]
    return pl.pallas_call(
        decode_kernel,
        in_specs=[whole(), whole(), *[in_hbm()] * PARTS],
        out_specs=[whole(), whole(), whole()],
        out_shape=[
            jax.ShapeDtypeStruct((tokens, wide), BF),
            jax.ShapeDtypeStruct((tokens, latents), BF),
            jax.ShapeDtypeStruct((tokens, latents), F32),
        ],
        scratch_shapes=[pltpu.VMEM((wide, latents), BF), pltpu.SemaphoreType.DMA((PARTS,))],
        compiler_params=params(50),
        cost_estimate=pl.CostEstimate(
            flops=2 * tokens * latents * wide,
            bytes_accessed=2 * wide * (latents + tokens),
            transcendentals=3 * tokens * latents,
        ),
        name="decode",
    )(quarter, enc_bias.reshape(1, latents), *dec_blocks)


def row_sum(rows, first, last):
    row = lax.broadcasted_iota(jnp.int32, rows.shape, 0)
    return jnp.sum(jnp.where((row >= first) & (row < last), rows, 0.0), axis=0, keepdims=True)


def error_kernel(scale, got_ref, mask_ref, *refs):
    *extra_refs, out_ref = refs
    small, longer = got_ref.shape[1:]
    wide = longer - LANES
    target = []
    for extra_ref in extra_refs:
        extra = extra_ref[...][0].astype(F32)
        left = wide // CHIPS - extra.shape[1]
        biases = extra[2 * small :]
        target.append(extra[:small] - row_sum(biases, 0, 3))
        target.append((extra[small : 2 * small] - row_sum(biases, 3, 6))[:, :left])
    total = jnp.sum(got_ref[...].astype(F32), axis=0)
    error = total[:, :wide] - jnp.concatenate(target, axis=1)
    squares = jnp.zeros((small, LANES), F32)
    for start in range(0, wide, LANES):
        part = error[:, start : start + LANES]
        squares = squares + part * part
    lanes = scale * (mask_ref[...] * squares + sparsity * total[:, wide:])
    row = jnp.concatenate([error * (2.0 * scale), lanes], axis=1).astype(BF)
    out_ref[...] = jnp.broadcast_to(row[None], out_ref.shape)


def error_copies(got, extras, mask, scale):
    rows, longer = got.shape[1:]
    return pl.pallas_call(
        functools.partial(error_kernel, scale),
        out_shape=jax.ShapeDtypeStruct((BLOCKS, rows, longer), BF),
        compiler_params=params(16),
        cost_estimate=pl.CostEstimate(
            flops=10 * rows * longer, bytes_accessed=60 * rows * longer, transcendentals=0
        ),
        name="error",
    )(got, mask, *extras)


def back_kernel(scale, grad_ref, slopes_ref, norms_ref, *refs):
    *dec_refs, out_ref, held, sems = refs
    wide, latents = held.shape
    step = wide // CHIPS
    blocks = start_blocks(dec_refs, held, sems)
    sums = jnp.sum(grad_ref[:, wide:].astype(F32), axis=0, keepdims=True)
    high, low = pieces(sums, 2)
    row = lax.broadcasted_iota(jnp.int32, (8, LANES), 0)
    both = jnp.where(row == 0, high.astype(F32), jnp.where(row == 1, low.astype(F32), 0.0))
    block = jnp.concatenate([both, jnp.zeros((8, latents - LANES), F32)], axis=1)
    code_grad = sparsity * scale * norms_ref[...]
    for k in range(CHIPS):
        await_chip(blocks, k)
        code_grad = code_grad + jnp.dot(
            grad_ref[:, k * step : (k + 1) * step],
            held[k * step : (k + 1) * step],
            preferred_element_type=F32,
        )
    out_ref[...] = jnp.concatenate([code_grad * slopes_ref[...], block], axis=0).astype(BF)


def back(grads, dec_blocks, slopes, norms, scale):
    tokens = grads.shape[0]
    wide, latents = PARTS * dec_blocks[0].shape[0], dec_blocks[0].shape[1]
    return pl.pallas_call(
        functools.partial(back_kernel, scale),
        in_specs=[whole(), whole(), whole(), *[in_hbm()] * PARTS],
        out_specs=whole(),
        out_shape=jax.ShapeDtypeStruct((tokens + 8, latents), BF),
        scratch_shapes=[pltpu.VMEM((wide, latents), BF), pltpu.SemaphoreType.DMA((PARTS,))],
        compiler_params=params(50),
        cost_estimate=pl.CostEstimate(
            flops=2 * tokens * latents * wide,
            bytes_accessed=2 * wide * (latents + tokens),
            transcendentals=0,
        ),
        name="back",
    )(grads, slopes, norms.reshape(1, latents), *dec_blocks)


def body(acts, enc_weight, enc_bias, dec_weight, dec_bias, enc_moment, enc_second):
    rows, chans = acts.shape
    latents = enc_weight.shape[1]
    inv_batch = 1.0 / (rows * BLOCKS * HIGH)
    wide = PARTS * chans
    core = lax.axis_index("core")
    chip = lax.axis_index("zl")
    share = (rows + 1) // PARTS
    half = CHIPS * share
    small = HIGH * share
    tokens = BLOCKS * small

    def shifted(value, away):
        return lax.ppermute(value, "zl", [(i, (i + away) % CHIPS) for i in range(CHIPS)])

    dec_own = dec_weight.T
    dec_first, dec_last = shifted(dec_own, 1), shifted(dec_own, CHIPS - 1)
    bias_here = jnp.stack(pieces(dec_bias, 3))
    bias_block = jnp.pad(bias_here, ((0, 13), (0, latents - chans)))
    swapped = swap(jnp.concatenate([enc_weight, dec_own, bias_block], axis=0))
    enc_there, bias_there = swapped[:chans], swapped[2 * chans : 2 * chans + 3, :chans]

    padded = jnp.concatenate([acts, jnp.zeros((1, chans), BF)], axis=0)
    halves = jnp.broadcast_to(padded.reshape(CORES, 1, half, chans), (CORES, HIGH, half, chans))
    halves = halves.reshape(CORES * HIGH, half, chans)
    column = lax.all_to_all(halves, ("core", "zh"), 0, 0, tiled=True)
    column = column.reshape(CORES, HIGH, CHIPS, share, chans)
    column = jnp.where(core == 0, column, column[::-1])
    column = column.transpose(2, 1, 3, 0, 4)
    column = column.reshape(CHIPS, small, 2 * chans)
    column, dec_first = lax.optimization_barrier((column, dec_first))
    dec_second = shifted(dec_first, 1)
    gathered = spread(column, PLANE, BLOCKS).transpose(1, 0, 2, 3)
    gathered = gathered.reshape(CHIPS * tokens, 2 * chans)

    acts_here = gathered[:, :chans]
    acts_there = swap(gathered[:, chans:])
    enc_pair = jnp.concatenate([enc_weight, enc_there], axis=0)
    sums = jnp.dot(gathered, enc_pair, preferred_element_type=F32).astype(BF)
    sums, dec_second, dec_last = lax.optimization_barrier((sums, dec_second, dec_last))
    dec_blocks = [dec_own, swapped]
    for block in (dec_first, dec_second, dec_last):
        dec_blocks += [block, swap(block)]
    quarter = lax.all_to_all(sums.reshape(CHIPS, tokens, latents), "zl", 0, 0, tiled=True)
    partial_value, codes, slopes = decode(quarter, enc_bias, dec_blocks, tokens)

    column, partial_value = lax.optimization_barrier((column, partial_value))
    def folded(rows_of):
        fill = [(0, 0)] * (rows_of.ndim - 1) + [(0, 2 * latents - 2 * chans)]
        rest = jnp.pad(rows_of[..., latents:], fill)
        return jnp.concatenate([rows_of[..., :latents], rest], axis=-2)

    bias_rows = folded(jnp.concatenate([bias_here, bias_there], axis=1))
    bias_rows = jnp.pad(bias_rows, ((0, small - 6), (0, 0)))
    bias_rows = jnp.broadcast_to(bias_rows[None], (CHIPS, small, latents))
    extra = jnp.concatenate([folded(column), bias_rows], axis=1)
    mine = []
    for away in range(CHIPS):
        block = lax.dynamic_index_in_dim(extra, (chip + away) & (CHIPS - 1), 0)
        mine.append(shifted(block, away) if away else block)

    def squares(block):
        block = block.astype(F32)
        return jnp.sum(block * block, axis=0)

    per_layer = [jnp.zeros((latents,), F32)] * LAYERS
    for away in range(CHIPS):
        near, far = dec_blocks[2 * away], dec_blocks[2 * away + 1]
        far = far if away else far[chans : 2 * chans]
        found = squares(near) + squares(far)
        layer = ((chip - away) & (CHIPS - 1)) // (CHIPS // LAYERS)
        per_layer = [t + jnp.where(layer == k, found, 0.0) for k, t in enumerate(per_layer)]
    dec_norms = sum(jnp.sqrt(t) for t in per_layer)

    place = lax.broadcasted_iota(jnp.int32, (small, LANES), 0) & (share - 1)
    real = (core * half + chip * share + place < rows).astype(F32)
    weighed = jnp.sum((codes.astype(F32) * dec_norms).reshape(BLOCKS, small, latents), axis=0)
    sparse = real * sum(weighed[:, k : k + LANES] for k in range(0, latents, LANES))

    got = lax.all_to_all(
        partial_value.reshape(BLOCKS, small, wide), PLANE, 0, 0, tiled=True
    )
    summed = jnp.sum(got.astype(F32), axis=0).astype(BF)
    again = spread(jnp.concatenate([summed, sparse.astype(BF)], axis=1), "zh", HIGH)
    again, acts_there = lax.optimization_barrier((again, acts_there))
    copies = error_copies(again, mine, real, inv_batch)
    grads = lax.all_to_all(copies, PLANE, 0, 0, tiled=True)
    last = back(grads.reshape(tokens, wide + LANES), dec_blocks, slopes, dec_norms, inv_batch)
    pre_here = lax.all_gather(last, "zl", axis=0)
    pre_there = swap(pre_here)

    def part_of(acts_half, pre_half):
        longer = jnp.pad(acts_half.reshape(CHIPS, tokens, chans), ((0, 0), (0, 8), (0, 0)))
        return lax.dot_general(
            longer.reshape(-1, chans),
            pre_half.reshape(-1, latents),
            (((0,), (0,)), ((), ())),
            preferred_element_type=F32,
        )

    near = pre_here[:, tokens : tokens + 2, :LANES].astype(F32)
    far = pre_there[:, tokens : tokens + 2, :LANES].astype(F32)
    first, second = jnp.where(core == 0, near, far), jnp.where(core == 0, far, near)
    total_loss = jnp.sum(first + second)
    gradient = part_of(acts_here, pre_here) + part_of(acts_there, pre_there)
    moment_new = beta_one * enc_moment + (1.0 - beta_one) * gradient
    second_new = beta_two * enc_second + (1.0 - beta_two) * gradient * gradient
    update = moment_new / first_fix / (jnp.sqrt(second_new / second_fix) + adam_eps)
    enc_new = (enc_weight.astype(F32) - learn_rate * update).astype(BF)
    return (enc_new, moment_new, second_new, total_loss)


def solution(mesh):
    fine = Mesh(mesh.devices.reshape(SIZES), NAMES)
    return jax.shard_map(
        body,
        mesh=fine,
        in_specs=(
            P(FEAT, LAYER),
            P(LAYER, FEAT),
            P(FEAT),
            P(FEAT, LAYER),
            P(LAYER),
            P(LAYER, FEAT),
            P(LAYER, FEAT),
        ),
        out_specs=(P(LAYER, FEAT), P(LAYER, FEAT), P(LAYER, FEAT), P()),
        check_vma=False,
    )
```

```python
import functools

import jax
import jax.numpy as jnp
from jax import lax
from jax.experimental import pallas as pl
from jax.experimental.pallas import tpu as pltpu
from jax.sharding import Mesh, PartitionSpec as P

D = 1792
LAYERS = 2

sparsity = 0.5
beta_one = 0.9
beta_two = 0.999
first_fix = 0.9999734386011124
second_fix = 0.0952078528862911
learn_rate = 0.002
adam_eps = 1e-08
sharpness = 4.0

SIZES = (4, 2, 4, 4, 4)
NAMES = ("zl", "core", "y", "x", "zh")
LAYER = ("zl", "core")
FEAT = ("y", "x", "zh")
PLANE = ("y", "x")
CORES = 2
CHIPS = 4
PARTS = 8
BLOCKS = 16
HIGH = 4
LANES = 128
BF = jnp.bfloat16
F32 = jnp.float32


def pieces(value, count):
    found = []
    for _ in range(count):
        top = value.astype(BF)
        found.append(top)
        value = value - top.astype(F32)
    return found


def spread(value, axes, count):
    copies = jnp.broadcast_to(value[None], (count,) + value.shape)
    return lax.all_to_all(copies, axes, 0, 0, tiled=True)


def swap(value):
    return lax.ppermute(value, "core", [(0, 1), (1, 0)])


def params(mebibytes):
    return pltpu.CompilerParams(vmem_limit_bytes=mebibytes * 1024 * 1024)


def start_blocks(sources, held, sems):
    step = sources[0].shape[0]
    found = []
    for place, source in enumerate(sources):
        first = step if source.shape[0] > step else 0
        there = pl.ds(place * step, step)
        found.append(
            pltpu.make_async_copy(source.at[pl.ds(first, step)], held.at[there], sems.at[place])
        )
    for copy in found:
        copy.start()
    return found


def await_chip(blocks, chip):
    for copy in blocks[chip * CORES : (chip + 1) * CORES]:
        copy.wait()


def decode_kernel(quarter_ref, bias_ref, *refs):
    *dec_refs, out_ref, codes_ref, slopes_ref, held, sems = refs
    step = held.shape[0] // CHIPS
    blocks = start_blocks(dec_refs, held, sems)
    sums = jnp.sum(quarter_ref[...].astype(F32), axis=0)
    scaled = sharpness * (sums + bias_ref[...])
    small = jnp.exp(-jnp.abs(scaled))
    soft = jnp.maximum(scaled, 0.0) + jnp.log1p(small)
    codes_ref[...] = (soft / sharpness).astype(BF)
    slopes_ref[...] = jnp.where(scaled >= 0.0, 1.0, small) / (1.0 + small)
    for k in range(CHIPS):
        await_chip(blocks, k)
        out_ref[:, k * step : (k + 1) * step] = lax.dot_general(
            codes_ref[...],
            held[k * step : (k + 1) * step],
            (((1,), (1,)), ((), ())),
            preferred_element_type=F32,
        ).astype(BF)


def in_hbm():
    return pl.BlockSpec(memory_space=pltpu.HBM)


def whole():
    return pl.BlockSpec(memory_space=pltpu.VMEM)


def decode(quarter, enc_bias, dec_blocks, tokens):
    wide, latents = PARTS * dec_blocks[0].shape[0], dec_blocks[0].shape[1]
    return pl.pallas_call(
        decode_kernel,
        in_specs=[whole(), whole(), *[in_hbm()] * PARTS],
        out_specs=[whole(), whole(), whole()],
        out_shape=[
            jax.ShapeDtypeStruct((tokens, wide), BF),
            jax.ShapeDtypeStruct((tokens, latents), BF),
            jax.ShapeDtypeStruct((tokens, latents), F32),
        ],
        scratch_shapes=[pltpu.VMEM((wide, latents), BF), pltpu.SemaphoreType.DMA((PARTS,))],
        compiler_params=params(52),
        cost_estimate=pl.CostEstimate(
            flops=2 * tokens * latents * wide,
            bytes_accessed=2 * wide * (latents + tokens),
            transcendentals=3 * tokens * latents,
        ),
        name="decode",
    )(quarter, enc_bias.reshape(1, latents), *dec_blocks)


def row_sum(rows, first, last):
    row = lax.broadcasted_iota(jnp.int32, rows.shape, 0)
    return jnp.sum(jnp.where((row >= first) & (row < last), rows, 0.0), axis=0, keepdims=True)


def error_kernel(scale, got_ref, mask_ref, *refs):
    *extra_refs, out_ref = refs
    small, longer = got_ref.shape[1:]
    wide = longer - LANES
    target = []
    for extra_ref in extra_refs:
        extra = extra_ref[...][0].astype(F32)
        left = wide // CHIPS - extra.shape[1]
        biases = extra[2 * small :]
        target.append(extra[:small] - row_sum(biases, 0, 3))
        target.append((extra[small : 2 * small] - row_sum(biases, 3, 6))[:, :left])
    total = jnp.sum(got_ref[...].astype(F32), axis=0)
    error = total[:, :wide] - jnp.concatenate(target, axis=1)
    squares = jnp.zeros((small, LANES), F32)
    for start in range(0, wide, LANES):
        part = error[:, start : start + LANES]
        squares = squares + part * part
    lanes = scale * (mask_ref[...] * squares + sparsity * total[:, wide:])
    row = jnp.concatenate([error * (2.0 * scale), lanes], axis=1).astype(BF)
    out_ref[...] = jnp.broadcast_to(row[None], out_ref.shape)


def error_copies(got, extras, mask, scale):
    rows, longer = got.shape[1:]
    return pl.pallas_call(
        functools.partial(error_kernel, scale),
        out_shape=jax.ShapeDtypeStruct((BLOCKS, rows, longer), BF),
        compiler_params=params(16),
        cost_estimate=pl.CostEstimate(
            flops=10 * rows * longer, bytes_accessed=60 * rows * longer, transcendentals=0
        ),
        name="error",
    )(got, mask, *extras)


def back_kernel(scale, grad_ref, slopes_ref, norms_ref, *refs):
    *dec_refs, out_ref, held, sems = refs
    wide, latents = held.shape
    step = wide // CHIPS
    blocks = start_blocks(dec_refs, held, sems)
    sums = jnp.sum(grad_ref[:, wide:].astype(F32), axis=0, keepdims=True)
    high, low = pieces(sums, 2)
    row = lax.broadcasted_iota(jnp.int32, (8, LANES), 0)
    both = jnp.where(row == 0, high.astype(F32), jnp.where(row == 1, low.astype(F32), 0.0))
    block = jnp.concatenate([both, jnp.zeros((8, latents - LANES), F32)], axis=1)
    code_grad = sparsity * scale * norms_ref[...]
    for k in range(CHIPS):
        await_chip(blocks, k)
        code_grad = code_grad + jnp.dot(
            grad_ref[:, k * step : (k + 1) * step],
            held[k * step : (k + 1) * step],
            preferred_element_type=F32,
        )
    out_ref[...] = jnp.concatenate([code_grad * slopes_ref[...], block], axis=0).astype(BF)


def back(grads, dec_blocks, slopes, norms, scale):
    tokens = grads.shape[0]
    wide, latents = PARTS * dec_blocks[0].shape[0], dec_blocks[0].shape[1]
    return pl.pallas_call(
        functools.partial(back_kernel, scale),
        in_specs=[whole(), whole(), whole(), *[in_hbm()] * PARTS],
        out_specs=whole(),
        out_shape=jax.ShapeDtypeStruct((tokens + 8, latents), BF),
        scratch_shapes=[pltpu.VMEM((wide, latents), BF), pltpu.SemaphoreType.DMA((PARTS,))],
        compiler_params=params(52),
        cost_estimate=pl.CostEstimate(
            flops=2 * tokens * latents * wide,
            bytes_accessed=2 * wide * (latents + tokens),
            transcendentals=0,
        ),
        name="back",
    )(grads, slopes, norms.reshape(1, latents), *dec_blocks)


def body(acts, enc_weight, enc_bias, dec_weight, dec_bias, enc_moment, enc_second):
    rows, chans = acts.shape
    latents = enc_weight.shape[1]
    inv_batch = 1.0 / (rows * BLOCKS * HIGH)
    wide = PARTS * chans
    core = lax.axis_index("core")
    chip = lax.axis_index("zl")
    share = (rows + 1) // PARTS
    half = CHIPS * share
    small = HIGH * share
    tokens = BLOCKS * small

    def shifted(value, away):
        return lax.ppermute(value, "zl", [(i, (i + away) % CHIPS) for i in range(CHIPS)])

    dec_own = dec_weight.T
    dec_first, dec_last = shifted(dec_own, 1), shifted(dec_own, CHIPS - 1)
    bias_here = jnp.stack(pieces(dec_bias, 3))
    bias_block = jnp.pad(bias_here, ((0, 13), (0, latents - chans)))
    swapped = swap(jnp.concatenate([enc_weight, dec_own, bias_block], axis=0))
    enc_there, bias_there = swapped[:chans], swapped[2 * chans : 2 * chans + 3, :chans]

    padded = jnp.concatenate([acts, jnp.zeros((1, chans), BF)], axis=0)
    halves = jnp.broadcast_to(padded.reshape(CORES, 1, half, chans), (CORES, HIGH, half, chans))
    halves = halves.reshape(CORES * HIGH, half, chans)
    column = lax.all_to_all(halves, ("core", "zh"), 0, 0, tiled=True)
    column = column.reshape(CORES, HIGH, CHIPS, share, chans)
    column = jnp.where(core == 0, column, column[::-1])
    column = column.transpose(2, 1, 3, 0, 4)
    column = column.reshape(CHIPS, small, 2 * chans)
    dec_second = shifted(dec_first, 1)
    gathered = spread(column, PLANE, BLOCKS).transpose(1, 0, 2, 3)
    gathered = gathered.reshape(CHIPS * tokens, 2 * chans)

    acts_here = gathered[:, :chans]
    acts_there = swap(gathered[:, chans:])
    enc_pair = jnp.concatenate([enc_weight, enc_there], axis=0)
    sums = jnp.dot(gathered, enc_pair, preferred_element_type=F32).astype(BF)
    sums, dec_second, dec_last = lax.optimization_barrier((sums, dec_second, dec_last))
    dec_blocks = [dec_own, swapped]
    for block in (dec_first, dec_second, dec_last):
        dec_blocks += [block, swap(block)]
    quarter = lax.all_to_all(sums.reshape(CHIPS, tokens, latents), "zl", 0, 0, tiled=True)
    partial_value, codes, slopes = decode(quarter, enc_bias, dec_blocks, tokens)

    column, partial_value = lax.optimization_barrier((column, partial_value))
    def folded(rows_of):
        fill = [(0, 0)] * (rows_of.ndim - 1) + [(0, 2 * latents - 2 * chans)]
        rest = jnp.pad(rows_of[..., latents:], fill)
        return jnp.concatenate([rows_of[..., :latents], rest], axis=-2)

    bias_rows = folded(jnp.concatenate([bias_here, bias_there], axis=1))
    bias_rows = jnp.pad(bias_rows, ((0, small - 6), (0, 0)))
    bias_rows = jnp.broadcast_to(bias_rows[None], (CHIPS, small, latents))
    extra = jnp.concatenate([folded(column), bias_rows], axis=1)
    mine = []
    for away in range(CHIPS):
        block = lax.dynamic_index_in_dim(extra, (chip + away) & (CHIPS - 1), 0)
        mine.append(shifted(block, away) if away else block)

    def squares(block):
        block = block.astype(F32)
        return jnp.sum(block * block, axis=0)

    per_layer = [jnp.zeros((latents,), F32)] * LAYERS
    for away in range(CHIPS):
        near, far = dec_blocks[2 * away], dec_blocks[2 * away + 1]
        far = far if away else far[chans : 2 * chans]
        found = squares(near) + squares(far)
        layer = ((chip - away) & (CHIPS - 1)) // (CHIPS // LAYERS)
        per_layer = [t + jnp.where(layer == k, found, 0.0) for k, t in enumerate(per_layer)]
    dec_norms = sum(jnp.sqrt(t) for t in per_layer)

    place = lax.broadcasted_iota(jnp.int32, (small, LANES), 0) & (share - 1)
    real = (core * half + chip * share + place < rows).astype(F32)
    weighed = jnp.sum((codes.astype(F32) * dec_norms).reshape(BLOCKS, small, latents), axis=0)
    sparse = real * sum(weighed[:, k : k + LANES] for k in range(0, latents, LANES))

    got = lax.all_to_all(
        partial_value.reshape(BLOCKS, small, wide), PLANE, 0, 0, tiled=True
    )
    got, *mine = lax.optimization_barrier((got, *mine))
    summed = jnp.sum(got.astype(F32), axis=0).astype(BF)
    again = spread(jnp.concatenate([summed, sparse.astype(BF)], axis=1), "zh", HIGH)
    again, acts_there = lax.optimization_barrier((again, acts_there))
    copies = error_copies(again, mine, real, inv_batch)
    grads = lax.all_to_all(copies, PLANE, 0, 0, tiled=True)
    last = back(grads.reshape(tokens, wide + LANES), dec_blocks, slopes, dec_norms, inv_batch)
    pre_here = lax.all_gather(last, "zl", axis=0)
    pre_there = swap(pre_here)

    def part_of(acts_half, pre_half):
        longer = jnp.pad(acts_half.reshape(CHIPS, tokens, chans), ((0, 0), (0, 8), (0, 0)))
        return lax.dot_general(
            longer.reshape(-1, chans),
            pre_half.reshape(-1, latents),
            (((0,), (0,)), ((), ())),
            preferred_element_type=F32,
        )

    near = pre_here[:, tokens : tokens + 2, :LANES].astype(F32)
    far = pre_there[:, tokens : tokens + 2, :LANES].astype(F32)
    first, second = jnp.where(core == 0, near, far), jnp.where(core == 0, far, near)
    total_loss = jnp.sum(first + second)
    gradient = part_of(acts_here, pre_here) + part_of(acts_there, pre_there)
    moment_new = beta_one * enc_moment + (1.0 - beta_one) * gradient
    second_new = beta_two * enc_second + (1.0 - beta_two) * gradient * gradient
    update = moment_new / first_fix / (jnp.sqrt(second_new / second_fix) + adam_eps)
    enc_new = (enc_weight.astype(F32) - learn_rate * update).astype(BF)
    return (enc_new, moment_new, second_new, total_loss)


def solution(mesh):
    fine = Mesh(mesh.devices.reshape(SIZES), NAMES)
    return jax.shard_map(
        body,
        mesh=fine,
        in_specs=(
            P(FEAT, LAYER),
            P(LAYER, FEAT),
            P(FEAT),
            P(FEAT, LAYER),
            P(LAYER),
            P(LAYER, FEAT),
            P(LAYER, FEAT),
        ),
        out_specs=(P(LAYER, FEAT), P(LAYER, FEAT), P(LAYER, FEAT), P()),
        check_vma=False,
    )
```

```python
import functools

import jax
import jax.numpy as jnp
from jax import lax
from jax.experimental import pallas as pl
from jax.experimental.pallas import tpu as pltpu
from jax.sharding import Mesh, PartitionSpec as P

D = 1792
LAYERS = 2

sparsity = 0.5
beta_one = 0.9
beta_two = 0.999
first_fix = 0.9999734386011124
second_fix = 0.0952078528862911
learn_rate = 0.002
adam_eps = 1e-08
sharpness = 4.0

SIZES = (4, 2, 4, 4, 4)
NAMES = ("zl", "core", "y", "x", "zh")
LAYER = ("zl", "core")
FEAT = ("y", "x", "zh")
PLANE = ("y", "x")
CORES = 2
CHIPS = 4
PARTS = 8
BLOCKS = 16
HIGH = 4
LANES = 128
BF = jnp.bfloat16
F32 = jnp.float32


def pieces(value, count):
    found = []
    for _ in range(count):
        top = value.astype(BF)
        found.append(top)
        value = value - top.astype(F32)
    return found


def spread(value, axes, count):
    copies = jnp.broadcast_to(value[None], (count,) + value.shape)
    return lax.all_to_all(copies, axes, 0, 0, tiled=True)


def swap(value):
    return lax.ppermute(value, "core", [(0, 1), (1, 0)])


def params(mebibytes):
    return pltpu.CompilerParams(vmem_limit_bytes=mebibytes * 1024 * 1024)


def start_blocks(sources, held, sems):
    step = sources[0].shape[0]
    found = []
    for place, source in enumerate(sources):
        first = step if source.shape[0] > step else 0
        there = pl.ds(place * step, step)
        found.append(
            pltpu.make_async_copy(source.at[pl.ds(first, step)], held.at[there], sems.at[place])
        )
    for copy in found:
        copy.start()
    return found


def await_chip(blocks, chip):
    for copy in blocks[chip * CORES : (chip + 1) * CORES]:
        copy.wait()


def decode_kernel(quarter_ref, bias_ref, *refs):
    *dec_refs, out_ref, codes_ref, slopes_ref, held, sems = refs
    step = held.shape[0] // CHIPS
    blocks = start_blocks(dec_refs, held, sems)
    sums = jnp.sum(quarter_ref[...].astype(F32), axis=0)
    scaled = sharpness * (sums + bias_ref[...])
    small = jnp.exp(-jnp.abs(scaled))
    soft = jnp.maximum(scaled, 0.0) + jnp.log1p(small)
    codes_ref[...] = (soft / sharpness).astype(BF)
    slopes_ref[...] = jnp.where(scaled >= 0.0, 1.0, small) / (1.0 + small)
    for k in range(CHIPS):
        await_chip(blocks, k)
        out_ref[:, k * step : (k + 1) * step] = lax.dot_general(
            codes_ref[...],
            held[k * step : (k + 1) * step],
            (((1,), (1,)), ((), ())),
            preferred_element_type=F32,
        ).astype(BF)


def in_hbm():
    return pl.BlockSpec(memory_space=pltpu.HBM)


def whole():
    return pl.BlockSpec(memory_space=pltpu.VMEM)


def decode(quarter, enc_bias, dec_blocks, tokens):
    wide, latents = PARTS * dec_blocks[0].shape[0], dec_blocks[0].shape[1]
    return pl.pallas_call(
        decode_kernel,
        in_specs=[whole(), whole(), *[in_hbm()] * PARTS],
        out_specs=[whole(), whole(), whole()],
        out_shape=[
            jax.ShapeDtypeStruct((tokens, wide), BF),
            jax.ShapeDtypeStruct((tokens, latents), BF),
            jax.ShapeDtypeStruct((tokens, latents), F32),
        ],
        scratch_shapes=[pltpu.VMEM((wide, latents), BF), pltpu.SemaphoreType.DMA((PARTS,))],
        compiler_params=params(56),
        cost_estimate=pl.CostEstimate(
            flops=2 * tokens * latents * wide,
            bytes_accessed=2 * wide * (latents + tokens),
            transcendentals=3 * tokens * latents,
        ),
        name="decode",
    )(quarter, enc_bias.reshape(1, latents), *dec_blocks)


def row_sum(rows, first, last):
    row = lax.broadcasted_iota(jnp.int32, rows.shape, 0)
    return jnp.sum(jnp.where((row >= first) & (row < last), rows, 0.0), axis=0, keepdims=True)


def error_kernel(scale, got_ref, mask_ref, *refs):
    *extra_refs, out_ref = refs
    small, longer = got_ref.shape[1:]
    wide = longer - LANES
    target = []
    for extra_ref in extra_refs:
        extra = extra_ref[...][0].astype(F32)
        left = wide // CHIPS - extra.shape[1]
        biases = extra[2 * small :]
        target.append(extra[:small] - row_sum(biases, 0, 3))
        target.append((extra[small : 2 * small] - row_sum(biases, 3, 6))[:, :left])
    total = jnp.sum(got_ref[...].astype(F32), axis=0)
    error = total[:, :wide] - jnp.concatenate(target, axis=1)
    squares = jnp.zeros((small, LANES), F32)
    for start in range(0, wide, LANES):
        part = error[:, start : start + LANES]
        squares = squares + part * part
    lanes = scale * (mask_ref[...] * squares + sparsity * total[:, wide:])
    row = jnp.concatenate([error * (2.0 * scale), lanes], axis=1).astype(BF)
    out_ref[...] = jnp.broadcast_to(row[None], out_ref.shape)


def error_copies(got, extras, mask, scale):
    rows, longer = got.shape[1:]
    return pl.pallas_call(
        functools.partial(error_kernel, scale),
        out_shape=jax.ShapeDtypeStruct((BLOCKS, rows, longer), BF),
        compiler_params=params(16),
        cost_estimate=pl.CostEstimate(
            flops=10 * rows * longer, bytes_accessed=60 * rows * longer, transcendentals=0
        ),
        name="error",
    )(got, mask, *extras)


def back_kernel(scale, grad_ref, slopes_ref, norms_ref, *refs):
    *dec_refs, out_ref, held, sems = refs
    wide, latents = held.shape
    step = wide // CHIPS
    blocks = start_blocks(dec_refs, held, sems)
    sums = jnp.sum(grad_ref[:, wide:].astype(F32), axis=0, keepdims=True)
    high, low = pieces(sums, 2)
    row = lax.broadcasted_iota(jnp.int32, (8, LANES), 0)
    both = jnp.where(row == 0, high.astype(F32), jnp.where(row == 1, low.astype(F32), 0.0))
    block = jnp.concatenate([both, jnp.zeros((8, latents - LANES), F32)], axis=1)
    code_grad = sparsity * scale * norms_ref[...]
    for k in range(CHIPS):
        await_chip(blocks, k)
        code_grad = code_grad + jnp.dot(
            grad_ref[:, k * step : (k + 1) * step],
            held[k * step : (k + 1) * step],
            preferred_element_type=F32,
        )
    out_ref[...] = jnp.concatenate([code_grad * slopes_ref[...], block], axis=0).astype(BF)


def back(grads, dec_blocks, slopes, norms, scale):
    tokens = grads.shape[0]
    wide, latents = PARTS * dec_blocks[0].shape[0], dec_blocks[0].shape[1]
    return pl.pallas_call(
        functools.partial(back_kernel, scale),
        in_specs=[whole(), whole(), whole(), *[in_hbm()] * PARTS],
        out_specs=whole(),
        out_shape=jax.ShapeDtypeStruct((tokens + 8, latents), BF),
        scratch_shapes=[pltpu.VMEM((wide, latents), BF), pltpu.SemaphoreType.DMA((PARTS,))],
        compiler_params=params(56),
        cost_estimate=pl.CostEstimate(
            flops=2 * tokens * latents * wide,
            bytes_accessed=2 * wide * (latents + tokens),
            transcendentals=0,
        ),
        name="back",
    )(grads, slopes, norms.reshape(1, latents), *dec_blocks)


def body(acts, enc_weight, enc_bias, dec_weight, dec_bias, enc_moment, enc_second):
    rows, chans = acts.shape
    latents = enc_weight.shape[1]
    inv_batch = 1.0 / (rows * BLOCKS * HIGH)
    wide = PARTS * chans
    core = lax.axis_index("core")
    chip = lax.axis_index("zl")
    share = (rows + 1) // PARTS
    half = CHIPS * share
    small = HIGH * share
    tokens = BLOCKS * small

    def shifted(value, away):
        return lax.ppermute(value, "zl", [(i, (i + away) % CHIPS) for i in range(CHIPS)])

    dec_own = dec_weight.T
    dec_first = shifted(dec_own, 1)
    bias_here = jnp.stack(pieces(dec_bias, 3))
    bias_block = jnp.pad(bias_here, ((0, 13), (0, latents - chans)))
    swapped = swap(jnp.concatenate([enc_weight, dec_own, bias_block], axis=0))
    enc_there, bias_there = swapped[:chans], swapped[2 * chans : 2 * chans + 3, :chans]

    padded = jnp.concatenate([acts, jnp.zeros((1, chans), BF)], axis=0)
    halves = jnp.broadcast_to(padded.reshape(CORES, 1, half, chans), (CORES, HIGH, half, chans))
    halves = halves.reshape(CORES * HIGH, half, chans)
    column = lax.all_to_all(halves, ("core", "zh"), 0, 0, tiled=True)
    column = column.reshape(CORES, HIGH, CHIPS, share, chans)
    column = jnp.where(core == 0, column, column[::-1])
    column = column.transpose(2, 1, 3, 0, 4)
    column = column.reshape(CHIPS, small, 2 * chans)
    dec_second = shifted(dec_first, 1)
    dec_last = shifted(dec_second, 1)
    gathered = spread(column, PLANE, BLOCKS).transpose(1, 0, 2, 3)
    gathered = gathered.reshape(CHIPS * tokens, 2 * chans)

    acts_here = gathered[:, :chans]
    acts_there = swap(gathered[:, chans:])
    enc_pair = jnp.concatenate([enc_weight, enc_there], axis=0)
    sums = jnp.dot(gathered, enc_pair, preferred_element_type=F32).astype(BF)
    sums, dec_second, dec_last = lax.optimization_barrier((sums, dec_second, dec_last))
    dec_blocks = [dec_own, swapped]
    for block in (dec_first, dec_second, dec_last):
        dec_blocks += [block, swap(block)]
    quarter = lax.all_to_all(sums.reshape(CHIPS, tokens, latents), "zl", 0, 0, tiled=True)
    partial_value, codes, slopes = decode(quarter, enc_bias, dec_blocks, tokens)

    column, partial_value = lax.optimization_barrier((column, partial_value))
    def folded(rows_of):
        fill = [(0, 0)] * (rows_of.ndim - 1) + [(0, 2 * latents - 2 * chans)]
        rest = jnp.pad(rows_of[..., latents:], fill)
        return jnp.concatenate([rows_of[..., :latents], rest], axis=-2)

    bias_rows = folded(jnp.concatenate([bias_here, bias_there], axis=1))
    bias_rows = jnp.pad(bias_rows, ((0, small - 6), (0, 0)))
    bias_rows = jnp.broadcast_to(bias_rows[None], (CHIPS, small, latents))
    extra = jnp.concatenate([folded(column), bias_rows], axis=1)
    mine = []
    for away in range(CHIPS):
        block = lax.dynamic_index_in_dim(extra, (chip + away) & (CHIPS - 1), 0)
        mine.append(shifted(block, away) if away else block)

    def squares(block):
        block = block.astype(F32)
        return jnp.sum(block * block, axis=0)

    per_layer = [jnp.zeros((latents,), F32)] * LAYERS
    for away in range(CHIPS):
        near, far = dec_blocks[2 * away], dec_blocks[2 * away + 1]
        far = far if away else far[chans : 2 * chans]
        found = squares(near) + squares(far)
        layer = ((chip - away) & (CHIPS - 1)) // (CHIPS // LAYERS)
        per_layer = [t + jnp.where(layer == k, found, 0.0) for k, t in enumerate(per_layer)]
    dec_norms = sum(jnp.sqrt(t) for t in per_layer)

    place = lax.broadcasted_iota(jnp.int32, (small, LANES), 0) & (share - 1)
    real = (core * half + chip * share + place < rows).astype(F32)
    weighed = jnp.sum((codes.astype(F32) * dec_norms).reshape(BLOCKS, small, latents), axis=0)
    sparse = real * sum(weighed[:, k : k + LANES] for k in range(0, latents, LANES))

    got = lax.all_to_all(
        partial_value.reshape(BLOCKS, small, wide), PLANE, 0, 0, tiled=True
    )
    got, *mine = lax.optimization_barrier((got, *mine))
    summed = jnp.sum(got.astype(F32), axis=0).astype(BF)
    again = spread(jnp.concatenate([summed, sparse.astype(BF)], axis=1), "zh", HIGH)
    again, acts_there = lax.optimization_barrier((again, acts_there))
    copies = error_copies(again, mine, real, inv_batch)
    grads = lax.all_to_all(copies, PLANE, 0, 0, tiled=True)
    last = back(grads.reshape(tokens, wide + LANES), dec_blocks, slopes, dec_norms, inv_batch)
    pre_here = lax.all_gather(last, "zl", axis=0)
    pre_there = swap(pre_here)

    def part_of(acts_half, pre_half):
        longer = jnp.pad(acts_half.reshape(CHIPS, tokens, chans), ((0, 0), (0, 8), (0, 0)))
        return lax.dot_general(
            longer.reshape(-1, chans),
            pre_half.reshape(-1, latents),
            (((0,), (0,)), ((), ())),
            preferred_element_type=F32,
        )

    near = pre_here[:, tokens : tokens + 2, :LANES].astype(F32)
    far = pre_there[:, tokens : tokens + 2, :LANES].astype(F32)
    first, second = jnp.where(core == 0, near, far), jnp.where(core == 0, far, near)
    total_loss = jnp.sum(first + second)
    gradient = part_of(acts_here, pre_here) + part_of(acts_there, pre_there)
    moment_new = beta_one * enc_moment + (1.0 - beta_one) * gradient
    second_new = beta_two * enc_second + (1.0 - beta_two) * gradient * gradient
    update = moment_new / first_fix / (jnp.sqrt(second_new / second_fix) + adam_eps)
    enc_new = (enc_weight.astype(F32) - learn_rate * update).astype(BF)
    return (enc_new, moment_new, second_new, total_loss)


def solution(mesh):
    fine = Mesh(mesh.devices.reshape(SIZES), NAMES)
    return jax.shard_map(
        body,
        mesh=fine,
        in_specs=(
            P(FEAT, LAYER),
            P(LAYER, FEAT),
            P(FEAT),
            P(FEAT, LAYER),
            P(LAYER),
            P(LAYER, FEAT),
            P(LAYER, FEAT),
        ),
        out_specs=(P(LAYER, FEAT), P(LAYER, FEAT), P(LAYER, FEAT), P()),
        check_vma=False,
    )
```

```python
import functools

import jax
import jax.numpy as jnp
from jax import lax
from jax.experimental import pallas as pl
from jax.experimental.pallas import tpu as pltpu
from jax.sharding import Mesh, PartitionSpec as P

D = 1792
LAYERS = 2

sparsity = 0.5
beta_one = 0.9
beta_two = 0.999
first_fix = 0.9999734386011124
second_fix = 0.0952078528862911
learn_rate = 0.002
adam_eps = 1e-08
sharpness = 4.0

SIZES = (4, 2, 4, 4, 4)
NAMES = ("zl", "core", "y", "x", "zh")
LAYER = ("zl", "core")
FEAT = ("y", "x", "zh")
PLANE = ("y", "x")
CORES = 2
CHIPS = 4
PARTS = 8
BLOCKS = 16
HIGH = 4
LANES = 128
BF = jnp.bfloat16
F32 = jnp.float32


def pieces(value, count):
    found = []
    for _ in range(count):
        top = value.astype(BF)
        found.append(top)
        value = value - top.astype(F32)
    return found


def spread(value, axes, count):
    copies = jnp.broadcast_to(value[None], (count,) + value.shape)
    return lax.all_to_all(copies, axes, 0, 0, tiled=True)


def swap(value):
    return lax.ppermute(value, "core", [(0, 1), (1, 0)])


def params(mebibytes):
    return pltpu.CompilerParams(vmem_limit_bytes=mebibytes * 1024 * 1024)


def start_blocks(source, held, sems, count):
    step = source.shape[0] // count
    found = []
    for k in range(count):
        rows = pl.ds(k * step, step)
        found.append(pltpu.make_async_copy(source.at[rows], held.at[rows], sems.at[k]))
    for copy in found:
        copy.start()
    return found


def decode_kernel(quarter_ref, bias_ref, dec_ref, out_ref, codes_ref, slopes_ref, held, sems):
    step = held.shape[0] // CHIPS
    blocks = start_blocks(dec_ref, held, sems, CHIPS)
    sums = jnp.sum(quarter_ref[...].astype(F32), axis=0)
    scaled = sharpness * (sums + bias_ref[...])
    small = jnp.exp(-jnp.abs(scaled))
    soft = jnp.maximum(scaled, 0.0) + jnp.log1p(small)
    codes_ref[...] = (soft / sharpness).astype(BF)
    slopes_ref[...] = jnp.where(scaled >= 0.0, 1.0, small) / (1.0 + small)
    for k in range(CHIPS):
        blocks[k].wait()
        out_ref[:, k * step : (k + 1) * step] = lax.dot_general(
            codes_ref[...],
            held[k * step : (k + 1) * step],
            (((1,), (1,)), ((), ())),
            preferred_element_type=F32,
        ).astype(BF)


def whole():
    return pl.BlockSpec(memory_space=pltpu.VMEM)


def decode(quarter, enc_bias, dec_all, tokens):
    wide, latents = dec_all.shape
    return pl.pallas_call(
        decode_kernel,
        in_specs=[whole(), whole(), pl.BlockSpec(memory_space=pltpu.HBM)],
        out_specs=[whole(), whole(), whole()],
        out_shape=[
            jax.ShapeDtypeStruct((tokens, wide), BF),
            jax.ShapeDtypeStruct((tokens, latents), BF),
            jax.ShapeDtypeStruct((tokens, latents), F32),
        ],
        scratch_shapes=[pltpu.VMEM((wide, latents), BF), pltpu.SemaphoreType.DMA((CHIPS,))],
        compiler_params=params(50),
        cost_estimate=pl.CostEstimate(
            flops=2 * tokens * latents * wide,
            bytes_accessed=2 * wide * (latents + tokens),
            transcendentals=3 * tokens * latents,
        ),
        name="decode",
    )(quarter, enc_bias.reshape(1, latents), dec_all)


def row_sum(rows, first, last):
    row = lax.broadcasted_iota(jnp.int32, rows.shape, 0)
    return jnp.sum(jnp.where((row >= first) & (row < last), rows, 0.0), axis=0, keepdims=True)


def error_kernel(scale, got_ref, extra_ref, mask_ref, out_ref):
    small, longer = got_ref.shape[1:]
    wide = longer - LANES
    left = wide // CHIPS - extra_ref.shape[2]
    extra = extra_ref[...].astype(F32)
    target = []
    for chip in range(CHIPS):
        biases = extra[chip, 2 * small :]
        target.append(extra[chip, :small] - row_sum(biases, 0, 3))
        target.append((extra[chip, small : 2 * small] - row_sum(biases, 3, 6))[:, :left])
    total = jnp.sum(got_ref[...].astype(F32), axis=0)
    error = total[:, :wide] - jnp.concatenate(target, axis=1)
    squares = jnp.zeros((small, LANES), F32)
    for start in range(0, wide, LANES):
        part = error[:, start : start + LANES]
        squares = squares + part * part
    lanes = scale * (mask_ref[...] * squares + sparsity * total[:, wide:])
    row = jnp.concatenate([error * (2.0 * scale), lanes], axis=1).astype(BF)
    out_ref[...] = jnp.broadcast_to(row[None], out_ref.shape)


def error_copies(got, extra, mask, scale):
    rows, longer = got.shape[1:]
    return pl.pallas_call(
        functools.partial(error_kernel, scale),
        out_shape=jax.ShapeDtypeStruct((BLOCKS, rows, longer), BF),
        compiler_params=params(16),
        cost_estimate=pl.CostEstimate(
            flops=10 * rows * longer, bytes_accessed=60 * rows * longer, transcendentals=0
        ),
        name="error",
    )(got, extra, mask)


def back_kernel(scale, grad_ref, dec_ref, slopes_ref, norms_ref, out_ref, held, sems):
    wide, latents = held.shape
    step = wide // CHIPS
    blocks = start_blocks(dec_ref, held, sems, CHIPS)
    sums = jnp.sum(grad_ref[:, wide:].astype(F32), axis=0, keepdims=True)
    high, low = pieces(sums, 2)
    row = lax.broadcasted_iota(jnp.int32, (8, LANES), 0)
    both = jnp.where(row == 0, high.astype(F32), jnp.where(row == 1, low.astype(F32), 0.0))
    block = jnp.concatenate([both, jnp.zeros((8, latents - LANES), F32)], axis=1)
    code_grad = sparsity * scale * norms_ref[...]
    for k in range(CHIPS):
        blocks[k].wait()
        code_grad = code_grad + jnp.dot(
            grad_ref[:, k * step : (k + 1) * step],
            held[k * step : (k + 1) * step],
            preferred_element_type=F32,
        )
    out_ref[...] = jnp.concatenate([code_grad * slopes_ref[...], block], axis=0).astype(BF)


def back(grads, dec_all, slopes, norms, scale):
    tokens = grads.shape[0]
    wide, latents = dec_all.shape
    return pl.pallas_call(
        functools.partial(back_kernel, scale),
        in_specs=[whole(), pl.BlockSpec(memory_space=pltpu.HBM), whole(), whole()],
        out_specs=whole(),
        out_shape=jax.ShapeDtypeStruct((tokens + 8, latents), BF),
        scratch_shapes=[pltpu.VMEM((wide, latents), BF), pltpu.SemaphoreType.DMA((CHIPS,))],
        compiler_params=params(50),
        cost_estimate=pl.CostEstimate(
            flops=2 * tokens * latents * wide,
            bytes_accessed=2 * wide * (latents + tokens),
            transcendentals=0,
        ),
        name="back",
    )(grads, dec_all, slopes, norms.reshape(1, latents))


def body(acts, enc_weight, enc_bias, dec_weight, dec_bias, enc_moment, enc_second):
    rows, chans = acts.shape
    latents = enc_weight.shape[1]
    inv_batch = 1.0 / (rows * BLOCKS * HIGH)
    wide = PARTS * chans
    core = lax.axis_index("core")
    chip = lax.axis_index("zl")
    share = (rows + 1) // PARTS
    half = CHIPS * share
    small = HIGH * share
    tokens = BLOCKS * small

    dec_all = lax.all_gather(dec_weight.T, LAYER, axis=0, tiled=True)
    enc_there = swap(enc_weight)
    bias_there = swap(dec_bias)

    def ordered(near, far, axis):
        first, second = jnp.where(core == 0, near, far), jnp.where(core == 0, far, near)
        return jnp.concatenate([first, second], axis=axis)

    padded = jnp.concatenate([acts, jnp.zeros((1, chans), BF)], axis=0)
    halves = jnp.broadcast_to(padded.reshape(CORES, 1, half, chans), (CORES, HIGH, half, chans))
    halves = halves.reshape(CORES * HIGH, half, chans)
    column = lax.all_to_all(halves, ("core", "zh"), 0, 0, tiled=True)
    column = column.reshape(CORES, HIGH, CHIPS, share, chans)

    def lined(blocks):
        return blocks.transpose(2, 1, 3, 0, 4).reshape(CHIPS, small, 2 * chans)

    own_first = lined(jnp.where(core == 0, column, column[::-1]))
    column = lined(column)
    gathered = spread(own_first, PLANE, BLOCKS).transpose(1, 0, 2, 3)
    gathered = gathered.reshape(CHIPS * tokens, 2 * chans)

    acts_here = gathered[:, :chans]
    acts_there = swap(gathered[:, chans:])
    enc_pair = jnp.concatenate([enc_weight, enc_there], axis=0)
    sums = jnp.dot(gathered, enc_pair, preferred_element_type=F32).astype(BF)
    quarter = lax.all_to_all(sums.reshape(CHIPS, tokens, latents), "zl", 0, 0, tiled=True)
    partial_value, codes, slopes = decode(quarter, enc_bias, dec_all, tokens)

    column, partial_value = lax.optimization_barrier((column, partial_value))

    def folded(rows_of):
        fill = [(0, 0)] * (rows_of.ndim - 1) + [(0, 2 * latents - 2 * chans)]
        rest = jnp.pad(rows_of[..., latents:], fill)
        return jnp.concatenate([rows_of[..., :latents], rest], axis=-2)

    bias_rows = folded(jnp.stack(pieces(ordered(dec_bias, bias_there, 0), 3)))
    bias_rows = jnp.pad(bias_rows, ((0, small - 6), (0, 0)))
    bias_rows = jnp.broadcast_to(bias_rows[None], (CHIPS, small, latents))
    extra = jnp.concatenate([folded(column), bias_rows], axis=1)
    came = []
    for away in range(CHIPS):
        block = lax.dynamic_index_in_dim(extra, (chip + away) & (CHIPS - 1), 0)
        ways = [(i, (i + away) % CHIPS) for i in range(CHIPS)]
        came.append(lax.ppermute(block, "zl", ways) if away else block)
    turned = jnp.concatenate([came[-k % CHIPS] for k in range(2 * CHIPS - 1)], axis=0)
    mine = lax.dynamic_slice_in_dim(turned, (CHIPS - chip) & (CHIPS - 1), CHIPS, axis=0)

    dec_norms = jnp.zeros((latents,), F32)
    for layer in range(LAYERS):
        block = dec_all[layer * (wide // LAYERS) : (layer + 1) * (wide // LAYERS)].astype(F32)
        dec_norms = dec_norms + jnp.sqrt(jnp.sum(block * block, axis=0))

    place = lax.broadcasted_iota(jnp.int32, (small, LANES), 0) & (share - 1)
    real = (core * half + chip * share + place < rows).astype(F32)
    weighed = jnp.sum((codes.astype(F32) * dec_norms).reshape(BLOCKS, small, latents), axis=0)
    sparse = real * sum(weighed[:, k : k + LANES] for k in range(0, latents, LANES))

    got = lax.all_to_all(
        partial_value.reshape(BLOCKS, small, wide), PLANE, 0, 0, tiled=True
    )
    got, mine = lax.optimization_barrier((got, mine))
    summed = jnp.sum(got.astype(F32), axis=0).astype(BF)
    again = spread(jnp.concatenate([summed, sparse.astype(BF)], axis=1), "zh", HIGH)
    again, acts_there = lax.optimization_barrier((again, acts_there))
    copies = error_copies(again, mine, real, inv_batch)
    grads = lax.all_to_all(copies, PLANE, 0, 0, tiled=True)
    last = back(grads.reshape(tokens, wide + LANES), dec_all, slopes, dec_norms, inv_batch)
    pre_here = lax.all_gather(last, "zl", axis=0)
    pre_there = swap(pre_here)

    def part_of(acts_half, pre_half):
        longer = jnp.pad(acts_half.reshape(CHIPS, tokens, chans), ((0, 0), (0, 8), (0, 0)))
        return lax.dot_general(
            longer.reshape(-1, chans),
            pre_half.reshape(-1, latents),
            (((0,), (0,)), ((), ())),
            preferred_element_type=F32,
        )

    near = pre_here[:, tokens : tokens + 2, :LANES].astype(F32)
    far = pre_there[:, tokens : tokens + 2, :LANES].astype(F32)
    first, second = jnp.where(core == 0, near, far), jnp.where(core == 0, far, near)
    total_loss = jnp.sum(first + second)
    gradient = part_of(acts_here, pre_here) + part_of(acts_there, pre_there)
    moment_new = beta_one * enc_moment + (1.0 - beta_one) * gradient
    second_new = beta_two * enc_second + (1.0 - beta_two) * gradient * gradient
    update = moment_new / first_fix / (jnp.sqrt(second_new / second_fix) + adam_eps)
    enc_new = (enc_weight.astype(F32) - learn_rate * update).astype(BF)
    return (enc_new, moment_new, second_new, total_loss)


def solution(mesh):
    fine = Mesh(mesh.devices.reshape(SIZES), NAMES)
    return jax.shard_map(
        body,
        mesh=fine,
        in_specs=(
            P(FEAT, LAYER),
            P(LAYER, FEAT),
            P(FEAT),
            P(FEAT, LAYER),
            P(LAYER),
            P(LAYER, FEAT),
            P(LAYER, FEAT),
        ),
        out_specs=(P(LAYER, FEAT), P(LAYER, FEAT), P(LAYER, FEAT), P()),
        check_vma=False,
    )
```

```python
import functools

import jax
import jax.numpy as jnp
from jax import lax
from jax.experimental import pallas as pl
from jax.experimental.pallas import tpu as pltpu
from jax.sharding import Mesh, PartitionSpec as P

D = 1792
LAYERS = 2

sparsity = 0.5
beta_one = 0.9
beta_two = 0.999
first_fix = 0.9999734386011124
second_fix = 0.0952078528862911
learn_rate = 0.002
adam_eps = 1e-08
sharpness = 4.0

SIZES = (4, 2, 4, 4, 4)
NAMES = ("zl", "core", "y", "x", "zh")
LAYER = ("zl", "core")
FEAT = ("y", "x", "zh")
PLANE = ("y", "x")
CORES = 2
CHIPS = 4
PARTS = 8
BLOCKS = 16
HIGH = 4
LANES = 128
BF = jnp.bfloat16
F32 = jnp.float32


def pieces(value, count):
    found = []
    for _ in range(count):
        top = value.astype(BF)
        found.append(top)
        value = value - top.astype(F32)
    return found


def spread(value, axes, count):
    copies = jnp.broadcast_to(value[None], (count,) + value.shape)
    return lax.all_to_all(copies, axes, 0, 0, tiled=True)


def swap(value):
    return lax.ppermute(value, "core", [(0, 1), (1, 0)])


def params(mebibytes):
    return pltpu.CompilerParams(vmem_limit_bytes=mebibytes * 1024 * 1024)


def start_blocks(source, held, sems, count):
    step = source.shape[0] // count
    found = []
    for k in range(count):
        rows = pl.ds(k * step, step)
        found.append(pltpu.make_async_copy(source.at[rows], held.at[rows], sems.at[k]))
    for copy in found:
        copy.start()
    return found


def decode_kernel(quarter_ref, bias_ref, dec_ref, out_ref, codes_ref, slopes_ref, held, sems):
    step = held.shape[0] // CHIPS
    blocks = start_blocks(dec_ref, held, sems, CHIPS)
    sums = jnp.sum(quarter_ref[...].astype(F32), axis=0)
    scaled = sharpness * (sums + bias_ref[...])
    small = jnp.exp(-jnp.abs(scaled))
    soft = jnp.maximum(scaled, 0.0) + jnp.log1p(small)
    codes_ref[...] = (soft / sharpness).astype(BF)
    slopes_ref[...] = jnp.where(scaled >= 0.0, 1.0, small) / (1.0 + small)
    for k in range(CHIPS):
        blocks[k].wait()
        out_ref[:, k * step : (k + 1) * step] = lax.dot_general(
            codes_ref[...],
            held[k * step : (k + 1) * step],
            (((1,), (1,)), ((), ())),
            preferred_element_type=F32,
        ).astype(BF)


def whole():
    return pl.BlockSpec(memory_space=pltpu.VMEM)


def decode(quarter, enc_bias, dec_all, tokens):
    wide, latents = dec_all.shape
    return pl.pallas_call(
        decode_kernel,
        in_specs=[whole(), whole(), pl.BlockSpec(memory_space=pltpu.HBM)],
        out_specs=[whole(), whole(), whole()],
        out_shape=[
            jax.ShapeDtypeStruct((tokens, wide), BF),
            jax.ShapeDtypeStruct((tokens, latents), BF),
            jax.ShapeDtypeStruct((tokens, latents), F32),
        ],
        scratch_shapes=[pltpu.VMEM((wide, latents), BF), pltpu.SemaphoreType.DMA((CHIPS,))],
        compiler_params=params(50),
        cost_estimate=pl.CostEstimate(
            flops=2 * tokens * latents * wide,
            bytes_accessed=2 * wide * (latents + tokens),
            transcendentals=3 * tokens * latents,
        ),
        name="decode",
    )(quarter, enc_bias.reshape(1, latents), dec_all)


def row_sum(rows, first, last):
    row = lax.broadcasted_iota(jnp.int32, rows.shape, 0)
    return jnp.sum(jnp.where((row >= first) & (row < last), rows, 0.0), axis=0, keepdims=True)


def error_kernel(scale, got_ref, extra_ref, mask_ref, out_ref):
    small, longer = got_ref.shape[1:]
    wide = longer - LANES
    left = wide // CHIPS - extra_ref.shape[2]
    extra = extra_ref[...].astype(F32)
    target = []
    for chip in range(CHIPS):
        biases = extra[chip, 2 * small :]
        target.append(extra[chip, :small] - row_sum(biases, 0, 3))
        target.append((extra[chip, small : 2 * small] - row_sum(biases, 3, 6))[:, :left])
    total = jnp.sum(got_ref[...].astype(F32), axis=0)
    error = total[:, :wide] - jnp.concatenate(target, axis=1)
    squares = jnp.zeros((small, LANES), F32)
    for start in range(0, wide, LANES):
        part = error[:, start : start + LANES]
        squares = squares + part * part
    lanes = scale * (mask_ref[...] * squares + sparsity * total[:, wide:])
    row = jnp.concatenate([error * (2.0 * scale), lanes], axis=1).astype(BF)
    out_ref[...] = jnp.broadcast_to(row[None], out_ref.shape)


def error_copies(got, extra, mask, scale):
    rows, longer = got.shape[1:]
    return pl.pallas_call(
        functools.partial(error_kernel, scale),
        out_shape=jax.ShapeDtypeStruct((BLOCKS, rows, longer), BF),
        compiler_params=params(16),
        cost_estimate=pl.CostEstimate(
            flops=10 * rows * longer, bytes_accessed=60 * rows * longer, transcendentals=0
        ),
        name="error",
    )(got, extra, mask)


def back_kernel(scale, grad_ref, dec_ref, slopes_ref, norms_ref, out_ref, held, sems):
    wide, latents = held.shape
    step = wide // CHIPS
    blocks = start_blocks(dec_ref, held, sems, CHIPS)
    sums = jnp.sum(grad_ref[:, wide:].astype(F32), axis=0, keepdims=True)
    high, low = pieces(sums, 2)
    row = lax.broadcasted_iota(jnp.int32, (8, LANES), 0)
    both = jnp.where(row == 0, high.astype(F32), jnp.where(row == 1, low.astype(F32), 0.0))
    block = jnp.concatenate([both, jnp.zeros((8, latents - LANES), F32)], axis=1)
    code_grad = sparsity * scale * norms_ref[...]
    for k in range(CHIPS):
        blocks[k].wait()
        code_grad = code_grad + jnp.dot(
            grad_ref[:, k * step : (k + 1) * step],
            held[k * step : (k + 1) * step],
            preferred_element_type=F32,
        )
    out_ref[...] = jnp.concatenate([code_grad * slopes_ref[...], block], axis=0).astype(BF)


def back(grads, dec_all, slopes, norms, scale):
    tokens = grads.shape[0]
    wide, latents = dec_all.shape
    return pl.pallas_call(
        functools.partial(back_kernel, scale),
        in_specs=[whole(), pl.BlockSpec(memory_space=pltpu.HBM), whole(), whole()],
        out_specs=whole(),
        out_shape=jax.ShapeDtypeStruct((tokens + 8, latents), BF),
        scratch_shapes=[pltpu.VMEM((wide, latents), BF), pltpu.SemaphoreType.DMA((CHIPS,))],
        compiler_params=params(50),
        cost_estimate=pl.CostEstimate(
            flops=2 * tokens * latents * wide,
            bytes_accessed=2 * wide * (latents + tokens),
            transcendentals=0,
        ),
        name="back",
    )(grads, dec_all, slopes, norms.reshape(1, latents))


def body(acts, enc_weight, enc_bias, dec_weight, dec_bias, enc_moment, enc_second):
    rows, chans = acts.shape
    latents = enc_weight.shape[1]
    inv_batch = 1.0 / (rows * BLOCKS * HIGH)
    wide = PARTS * chans
    core = lax.axis_index("core")
    chip = lax.axis_index("zl")
    share = (rows + 1) // PARTS
    half = CHIPS * share
    small = HIGH * share
    tokens = BLOCKS * small

    dec_all = lax.all_gather(dec_weight.T, LAYER, axis=0, tiled=True)
    enc_there = swap(enc_weight)
    bias_there = swap(dec_bias)

    def ordered(near, far, axis):
        first, second = jnp.where(core == 0, near, far), jnp.where(core == 0, far, near)
        return jnp.concatenate([first, second], axis=axis)

    padded = jnp.concatenate([acts, jnp.zeros((1, chans), BF)], axis=0)
    halves = jnp.broadcast_to(padded.reshape(CORES, 1, half, chans), (CORES, HIGH, half, chans))
    halves = halves.reshape(CORES * HIGH, half, chans)
    column = lax.all_to_all(halves, ("core", "zh"), 0, 0, tiled=True)
    column = column.reshape(CORES, HIGH, CHIPS, share, chans)

    def lined(blocks):
        return blocks.transpose(2, 1, 3, 0, 4).reshape(CHIPS, small, 2 * chans)

    own_first = lined(jnp.where(core == 0, column, column[::-1]))
    column = lined(column)
    gathered = spread(own_first, PLANE, BLOCKS).transpose(1, 0, 2, 3)
    gathered = gathered.reshape(CHIPS * tokens, 2 * chans)

    acts_here = gathered[:, :chans]
    acts_there = swap(gathered[:, chans:])
    enc_pair = jnp.concatenate([enc_weight, enc_there], axis=0)
    sums = jnp.dot(gathered, enc_pair, preferred_element_type=F32).astype(BF)
    quarter = lax.all_to_all(sums.reshape(CHIPS, tokens, latents), "zl", 0, 0, tiled=True)
    partial_value, codes, slopes = decode(quarter, enc_bias, dec_all, tokens)

    column, partial_value = lax.optimization_barrier((column, partial_value))

    def folded(rows_of):
        fill = [(0, 0)] * (rows_of.ndim - 1) + [(0, 2 * latents - 2 * chans)]
        rest = jnp.pad(rows_of[..., latents:], fill)
        return jnp.concatenate([rows_of[..., :latents], rest], axis=-2)

    bias_rows = folded(jnp.stack(pieces(ordered(dec_bias, bias_there, 0), 3)))
    bias_rows = jnp.pad(bias_rows, ((0, small - 6), (0, 0)))
    bias_rows = jnp.broadcast_to(bias_rows[None], (CHIPS, small, latents))
    extra = jnp.concatenate([folded(column), bias_rows], axis=1)
    came = []
    for away in range(CHIPS):
        block = lax.dynamic_index_in_dim(extra, (chip + away) & (CHIPS - 1), 0)
        ways = [(i, (i + away) % CHIPS) for i in range(CHIPS)]
        came.append(lax.ppermute(block, "zl", ways) if away else block)
    turned = jnp.concatenate([came[-k % CHIPS] for k in range(2 * CHIPS - 1)], axis=0)
    mine = lax.dynamic_slice_in_dim(turned, (CHIPS - chip) & (CHIPS - 1), CHIPS, axis=0)

    dec_norms = jnp.zeros((latents,), F32)
    for layer in range(LAYERS):
        block = dec_all[layer * (wide // LAYERS) : (layer + 1) * (wide // LAYERS)].astype(F32)
        dec_norms = dec_norms + jnp.sqrt(jnp.sum(block * block, axis=0))

    place = lax.broadcasted_iota(jnp.int32, (small, LANES), 0) & (share - 1)
    real = (core * half + chip * share + place < rows).astype(F32)
    weighed = jnp.sum((codes.astype(F32) * dec_norms).reshape(BLOCKS, small, latents), axis=0)
    sparse = real * sum(weighed[:, k : k + LANES] for k in range(0, latents, LANES))

    got = lax.all_to_all(
        partial_value.reshape(BLOCKS, small, wide), PLANE, 0, 0, tiled=True
    )
    got, mine = lax.optimization_barrier((got, mine))
    summed = jnp.sum(got.astype(F32), axis=0).astype(BF)
    again = lax.all_gather(jnp.concatenate([summed, sparse.astype(BF)], axis=1), "zh", axis=0)
    again, acts_there = lax.optimization_barrier((again, acts_there))
    copies = error_copies(again, mine, real, inv_batch)
    grads = lax.all_to_all(copies, PLANE, 0, 0, tiled=True)
    last = back(grads.reshape(tokens, wide + LANES), dec_all, slopes, dec_norms, inv_batch)
    pre_here = lax.all_gather(last, "zl", axis=0)
    pre_there = swap(pre_here)

    def part_of(acts_half, pre_half):
        longer = jnp.pad(acts_half.reshape(CHIPS, tokens, chans), ((0, 0), (0, 8), (0, 0)))
        return lax.dot_general(
            longer.reshape(-1, chans),
            pre_half.reshape(-1, latents),
            (((0,), (0,)), ((), ())),
            preferred_element_type=F32,
        )

    near = pre_here[:, tokens : tokens + 2, :LANES].astype(F32)
    far = pre_there[:, tokens : tokens + 2, :LANES].astype(F32)
    first, second = jnp.where(core == 0, near, far), jnp.where(core == 0, far, near)
    total_loss = jnp.sum(first + second)
    gradient = part_of(acts_here, pre_here) + part_of(acts_there, pre_there)
    moment_new = beta_one * enc_moment + (1.0 - beta_one) * gradient
    second_new = beta_two * enc_second + (1.0 - beta_two) * gradient * gradient
    update = moment_new / first_fix / (jnp.sqrt(second_new / second_fix) + adam_eps)
    enc_new = (enc_weight.astype(F32) - learn_rate * update).astype(BF)
    return (enc_new, moment_new, second_new, total_loss)


def solution(mesh):
    fine = Mesh(mesh.devices.reshape(SIZES), NAMES)
    return jax.shard_map(
        body,
        mesh=fine,
        in_specs=(
            P(FEAT, LAYER),
            P(LAYER, FEAT),
            P(FEAT),
            P(FEAT, LAYER),
            P(LAYER),
            P(LAYER, FEAT),
            P(LAYER, FEAT),
        ),
        out_specs=(P(LAYER, FEAT), P(LAYER, FEAT), P(LAYER, FEAT), P()),
        check_vma=False,
    )
```
